512 devices in a mesh: stn: 32 (over z_lo, y), tm: 16 (over z_hi, x, core).
Axes of the slice: x: 4, y: 4, z: 16 (z_hi: 2, z_lo: 8; z = z_hi * 8 + z_lo), core: 2. Of those that a mesh axis runs over, the one named last changes fastest.
Arguments:
- voltages: bfloat16 [2, 128, 393216], P(None, 'stn', 'tm'), may hold values from -20 to 20, as said below
Outputs:
- visibilities: float32 [2, 128, 128, 4096], P(None, 'stn', None, 'tm')
The draws below stay inside these ranges and needn't reach their ends.
Inputs may be any that keep to these rules, and one draw needn't show every extreme that they name: `voltages`: voltage samples.
All inputs are finite; a program needn't handle non-finite values.
Results may differ from the reference program's by a relative error of at most 0.0018.
Values may be sent and summed in bfloat16 or wider, within the bound.
No kernel may reach another device: no remote copies, remote signals or barrier semaphores. Data moves between devices by JAX's collectives and lax.ppermute only.
A program may use at most 128 MiB of HBM per device.

```python
import math
import jax
import jax.numpy as jnp
from jax import lax

TAPS = 16
RADIX = 64
NCH = 4096
STATIONS = 64
INPUTS = 128
FRAMES = 96
SAMPLES = 393216


def draw_voltages(key, part):
    key = jax.random.fold_in(key, 7)
    subkeys = jax.random.split(key, 4)
    lag_most = 2048
    sky_field = jax.random.truncated_normal(subkeys[0], -4.0, 4.0, (3, 2, 2, SAMPLES + lag_most), jnp.float32)
    delays = jax.random.randint(subkeys[1], (3, STATIONS), 0, lag_most)
    gain_table = jnp.exp(jax.random.uniform(subkeys[2], (3, INPUTS), jnp.float32, math.log(0.3), math.log(1.2)))
    summed = 0.5 * jax.random.truncated_normal(subkeys[3], -4.0, 4.0, (2, INPUTS, SAMPLES), jnp.float32)
    polar = (jnp.arange(INPUTS) % 2).astype(jnp.int32)
    for source in range(3):
        delay_in = jnp.repeat(delays[source], 2).astype(jnp.int32)
        field_now = sky_field[source]

        def window_cut(delay_one, polar_one):
            zero_at = jnp.zeros((), jnp.int32)
            return lax.dynamic_slice(field_now, (polar_one, zero_at, delay_one), (1, 2, SAMPLES))[0]
        delayed = jax.vmap(window_cut)(delay_in, polar)
        summed = summed + gain_table[source][None, :, None] * jnp.transpose(delayed, (1, 0, 2))
    return summed.astype(jnp.bfloat16)


def setup_inputs(seed: int = 0) -> dict:
    keys = jax.random.split(jax.random.key(seed), 2)
    voltages = draw_voltages(jax.random.fold_in(keys[1], 71), 0)
    return {"voltages": voltages}


def prototype():
    total = TAPS * NCH
    index = jnp.arange(total).astype(jnp.float32)
    offset = (index + 0.5 - total / 2.0) / NCH
    window = 0.5 - 0.5 * jnp.cos(2.0 * math.pi * (index + 0.5) / total)
    return (jnp.sinc(offset) * window).reshape(TAPS, NCH)


def reference(voltages):
    taps_table = prototype()

    def one_input(samples):
        framed = samples.astype(jnp.float32).reshape(2, FRAMES, NCH)
        padded = jnp.concatenate([jnp.zeros((2, TAPS - 1, NCH), jnp.float32), framed], 1)
        filtered = jnp.zeros((2, FRAMES, NCH), jnp.float32)
        for tap in range(TAPS):
            filtered = filtered + padded[:, tap:tap + FRAMES, :] * taps_table[tap]
        filtered = filtered.astype(jnp.bfloat16).astype(jnp.float32)
        signal = filtered[0] + 1j * filtered[1]
        spectrum = jnp.fft.fft(signal, axis=-1) / RADIX
        return jnp.stack([jnp.real(spectrum), jnp.imag(spectrum)]).astype(jnp.bfloat16)

    spectra = lax.map(one_input, jnp.transpose(voltages, (1, 0, 2)))
    block_width = min(256, NCH)
    blocks = NCH // block_width
    spectra = spectra.reshape(INPUTS, 2, FRAMES, blocks, block_width)
    spectra = jnp.transpose(spectra, (3, 0, 1, 2, 4))

    def one_block(block):
        values = block.astype(jnp.float32)
        products = jnp.einsum('iafc,jbfc->abijc', values, values, precision=lax.Precision.HIGHEST)
        real_part = products[0, 0] + products[1, 1]
        imag_part = products[1, 0] - products[0, 1]
        return jnp.stack([real_part, imag_part]) / FRAMES

    result = lax.map(one_block, spectra)
    return jnp.transpose(result, (1, 2, 3, 0, 4)).reshape(2, INPUTS, INPUTS, NCH)
```

```python
import math

import jax
import jax.numpy as jnp
import ml_dtypes
import numpy as np
from jax import lax
from jax.experimental import pallas as pl
from jax.experimental.pallas import tpu as pltpu
from jax.sharding import Mesh
from jax.sharding import PartitionSpec as P

TAPS = 16
NCH = 4096
N1, N2 = 32, 128
STN, ZH, Q = 32, 2, 8
FRAMES = 96
BLOCK = 24
HIST = TAPS - 1
SENT = 6
PER = 4
PARAMS = pltpu.CompilerParams(vmem_limit_bytes=48 * 1024 * 1024)
F32, BF16 = jnp.float32, jnp.bfloat16
NT = (((1,), (1,)), ((), ()))


def prototype():
    index = np.arange(TAPS * NCH, dtype=np.float64)
    window = 0.5 - 0.5 * np.cos(2.0 * math.pi * (index + 0.5) / (TAPS * NCH))
    taps = np.sinc((index + 0.5 - TAPS * NCH / 2) / NCH) * window
    return taps.astype(np.float32).reshape(TAPS, N1, N2)


def halves(table):
    high = table.astype(ml_dtypes.bfloat16)
    low = (table - high.astype(np.float64)).astype(ml_dtypes.bfloat16)
    return high, low


def complex_block(angle):
    c, s = np.cos(angle), np.sin(angle)
    return np.block([[c, s], [-s, c]])


def tables():
    k1, k2 = np.arange(N1), np.arange(N2)
    first = complex_block(2 * math.pi * (np.outer(k1, k1) % N1) / N1)
    second = complex_block(2 * math.pi * (np.outer(k2, k2) % N2) / N2) / 64.0
    second = second.reshape(2, ZH, Q, 8, 2 * N2).transpose(2, 1, 0, 3, 4).reshape(2 * N2, 2 * N2)
    turn = 2 * math.pi * np.outer(k1, k2) / NCH
    first = np.concatenate(halves(first), 0)
    second = np.concatenate(halves(second), 0)
    twiddle = np.stack([np.cos(turn), np.sin(turn)]).astype(np.float32)
    return first, second, twiddle


def channelise_body(core, main, hist, taps, first, second, twiddle, out, frames, stage, turned_re, turned_im):
    @pl.when(core[0] == 0)
    def _():
        for r in range(2):
            frames[r, :HIST] = hist[r].astype(F32)
            for s in range(4):
                frames[r, HIST + SENT * s : HIST + SENT * (s + 1)] = main[s, r].astype(F32)

    @pl.when(core[0] != 0)
    def _():
        for r in range(2):
            frames[r, :3] = main[1, r, 3:].astype(F32)
            for s in range(2, 8):
                frames[r, 3 + SENT * (s - 2) : 3 + SENT * (s - 1)] = main[s, r].astype(F32)

    def pair(step, carry):
        for half in range(2):
            f = 2 * step + half
            for r in range(2):
                acc = taps[0] * frames[r, f]
                for k in range(1, TAPS):
                    acc = acc + taps[k] * frames[r, f + k]
                stage[N1 * r : N1 * (r + 1), N2 * half : N2 * (half + 1)] = acc.astype(BF16)
        both = jnp.dot(first[...], stage[...], preferred_element_type=F32)
        both = both[: 2 * N1] + both[2 * N1 :]
        for half in range(2):
            re = both[:N1, N2 * half : N2 * (half + 1)]
            im = both[N1:, N2 * half : N2 * (half + 1)]
            f = 2 * step + half
            turned_re[pl.ds(f, N1, stride=BLOCK), :] = re * twiddle[0] + im * twiddle[1]
            turned_im[pl.ds(f, N1, stride=BLOCK), :] = im * twiddle[0] - re * twiddle[1]
        return carry

    lax.fori_loop(0, BLOCK // 2, pair, 0)
    for t in range(3):
        rows = slice(256 * t, 256 * (t + 1))
        value = jnp.concatenate([turned_re[rows], turned_im[rows]], 1)
        high = value.astype(BF16)
        low = (value - high.astype(F32)).astype(BF16)
        both = lax.dot_general(second[...], high, NT, preferred_element_type=F32)
        rest = lax.dot_general(second[: 2 * N2], low, NT, preferred_element_type=F32)
        out[:, rows] = (both[: 2 * N2] + (both[2 * N2 :] + rest)).astype(BF16)


def channelise(core, main, hist, interpret=False):
    first, second, twiddle = tables()
    args = (core, main, hist, prototype(), first, second, twiddle)
    vmem = pl.BlockSpec(memory_space=pltpu.VMEM)
    return pl.pallas_call(
        channelise_body,
        out_shape=jax.ShapeDtypeStruct((2 * N2, N1 * BLOCK), BF16),
        in_specs=[pl.BlockSpec(memory_space=pltpu.SMEM)] + [vmem] * 6,
        out_specs=vmem,
        scratch_shapes=[
            pltpu.VMEM((2, BLOCK + HIST, N1, N2), F32),
            pltpu.VMEM((2 * N1, 2 * N2), BF16),
            pltpu.VMEM((N1 * BLOCK, N2), F32),
            pltpu.VMEM((N1 * BLOCK, N2), F32),
        ],
        compiler_params=PARAMS,
        interpret=interpret,
        name="channelise",
    )(*[jnp.asarray(a) for a in args])


def regroup_body(x, out):
    for z in range(ZH):
        pieces = []
        for c in range(2):
            for r in range(2):
                for i in range(PER):
                    pair = x[2 * i + c, 16 * z : 16 * z + 16, :].astype(F32)
                    pieces.append(pair[8 * r : 8 * r + 8])
        for t in range(N1 * BLOCK // 128):
            piece = jnp.concatenate([p[:, 128 * t : 128 * (t + 1)] for p in pieces], 0).T
            for part in range(16):
                row = 128 * t + 8 * part
                out[row // BLOCK, z, row % BLOCK : row % BLOCK + 8, :] = piece[8 * part : 8 * part + 8].astype(BF16)


def regroup(x, interpret=False):
    vmem = pl.BlockSpec(memory_space=pltpu.VMEM)
    return pl.pallas_call(
        regroup_body,
        out_shape=jax.ShapeDtypeStruct((STN, ZH, BLOCK, 128), BF16),
        in_specs=[vmem],
        out_specs=vmem,
        compiler_params=PARAMS,
        interpret=interpret,
        name="regroup",
    )(x)


def correlate_body(x, out, series, plain):
    most = jnp.zeros((8, 128), F32)
    zero = jnp.zeros((128 - FRAMES, 128), F32)
    for s in range(STN):
        both = jnp.concatenate([x[s, 0].astype(F32), x[s, 1].astype(F32)], 0)
        cols = jnp.concatenate([both, pltpu.roll(both, 64, 1), zero], 0)
        series[64 * s : 64 * (s + 1), :] = cols.T[:64]
    sign = jnp.where(lax.broadcasted_iota(jnp.int32, (STN, 8, 128), 1) < PER, 1.0, -1.0)
    for j in range(8):
        near = series[pl.ds(j, 8 * STN, stride=8), :].reshape(STN, 8, 128)
        far = (pltpu.roll(near, PER, 1) * sign).reshape(8 * STN, 128)
        left = jnp.concatenate([near.reshape(8 * STN, 128), far], 1).astype(BF16)
        right = []
        for r in range(2):
            rows = [series[pl.ds(32 * r + 8 * i + j, STN, stride=64), :] for i in range(PER)]
            right.append(jnp.concatenate(rows, 0))
        right = jnp.concatenate(right, 1).astype(BF16)
        tile = lax.dot_general(left, right, NT, preferred_element_type=F32) / FRAMES
        tile = tile.reshape(STN, 8, 128)
        plain[:, 8 * j : 8 * j + 8, :] = tile
        most = jnp.maximum(most, jnp.max(jnp.abs(tile), 0))
    top = jnp.max(jnp.max(most, 1, keepdims=True), 0, keepdims=True)
    power = jnp.maximum(jnp.floor(jnp.log2(jnp.maximum(top, 1e-37))) - 14.0, -126.0)
    out[:, :64, :] = plain[...] * jnp.exp2(-power).reshape(1, 1, 1)
    out[:, 64:, :] = jnp.broadcast_to(power.reshape(1, 1, 1), (STN, 8, 128))


def correlate(x, interpret=False):
    vmem = pl.BlockSpec(memory_space=pltpu.VMEM)
    return pl.pallas_call(
        correlate_body,
        out_shape=jax.ShapeDtypeStruct((STN, 72, 128), F32),
        in_specs=[vmem],
        out_specs=vmem,
        scratch_shapes=[pltpu.VMEM((64 * STN, 128), F32), pltpu.VMEM((STN, 64, 128), F32)],
        compiler_params=PARAMS,
        interpret=interpret,
        name="correlate",
    )(x)


def deliver_body(x, out, wide, order):
    for k in range(N1):
        wide[64 * k : 64 * (k + 1), :] = x[k, :64, :] * jnp.exp2(x[k, 64:65, :])
    for row in range(8):
        for half in range(2):
            cols = jnp.concatenate(
                [wide[pl.ds(8 * j + row, N1, stride=64), :] for j in range(4 * half, 4 * half + 4)], 0
            ).T
            base = 128 * (2 * row + half)
            for i in range(PER):
                order[pl.ds(base + i, STN, stride=PER), :] = cols[STN * i : STN * (i + 1)]
            out[row // PER, row % PER, :, 128 * half : 128 * (half + 1)] = order[base : base + 128, :]


def deliver(x, interpret=False):
    vmem = pl.BlockSpec(memory_space=pltpu.VMEM)
    return pl.pallas_call(
        deliver_body,
        out_shape=jax.ShapeDtypeStruct((2, PER, 128, 256), F32),
        in_specs=[vmem],
        out_specs=vmem,
        scratch_shapes=[pltpu.VMEM((64 * N1, 128), F32), pltpu.VMEM((16 * 128, 128), F32)],
        compiler_params=PARAMS,
        interpret=interpret,
        name="deliver",
    )(x)


def shards(voltages):
    frames = voltages.reshape(2, PER, SENT, N1, N2).transpose(1, 0, 2, 3, 4)
    frames = jnp.repeat(frames, 2, 0)
    half = lax.all_to_all(frames, "q", 0, 0, tiled=True)
    last = jnp.concatenate([half[5, :, 3:], half[6], half[7]], 1)
    pairs = [((0 * Q + 2 * x), (1 * Q + 2 * x)) for x in range(Q // 2)]
    hist = lax.ppermute(last, ("zh", "q"), pairs)
    core = (lax.axis_index("q") % 2).astype(jnp.int32).reshape(1)
    spectra = channelise(core, half, hist)
    spectra = lax.all_to_all(spectra.reshape(Q, 2 * N2 // Q, N1 * BLOCK), "q", 0, 0, tiled=True)
    spectra = regroup(spectra).reshape(STN * ZH, BLOCK, 128)
    spectra = lax.all_to_all(spectra, ("stn", "zh"), 0, 0, tiled=True)
    products = correlate(spectra.reshape(STN, ZH, BLOCK, 128))
    products = lax.all_to_all(products.astype(jnp.float16), "stn", 0, 0, tiled=True)
    return deliver(products.astype(F32))


def solution(mesh):
    split = Mesh(mesh.devices.reshape(STN, ZH, Q), ("stn", "zh", "q"))
    in_specs = (P(None, "stn", ("zh", "q")),)
    out_specs = P(None, "stn", None, ("zh", "q"))
    return jax.shard_map(shards, mesh=split, in_specs=in_specs, out_specs=out_specs, check_vma=False)
```

```python
import math

import jax
import jax.numpy as jnp
import ml_dtypes
import numpy as np
from jax import lax
from jax.experimental import pallas as pl
from jax.experimental.pallas import tpu as pltpu
from jax.sharding import Mesh
from jax.sharding import PartitionSpec as P

TAPS = 16
NCH = 4096
N1, N2 = 32, 128
STN, ZH, X, Q = 32, 2, 4, 8
FRAMES = 96
BLOCK = 24
HIST = TAPS - 1
SENT = 6
PER = 4
PARAMS = pltpu.CompilerParams(vmem_limit_bytes=48 * 1024 * 1024)
F32, BF16 = jnp.float32, jnp.bfloat16
NT = (((1,), (1,)), ((), ()))


def prototype():
    index = np.arange(TAPS * NCH, dtype=np.float64)
    window = 0.5 - 0.5 * np.cos(2.0 * math.pi * (index + 0.5) / (TAPS * NCH))
    taps = np.sinc((index + 0.5 - TAPS * NCH / 2) / NCH) * window
    return taps.astype(np.float32).reshape(TAPS, N1, N2)


def halves(table):
    high = table.astype(ml_dtypes.bfloat16)
    low = (table - high.astype(np.float64)).astype(ml_dtypes.bfloat16)
    return high, low


def complex_block(angle):
    c, s = np.cos(angle), np.sin(angle)
    return np.block([[c, s], [-s, c]])


def tables():
    k1, k2 = np.arange(N1), np.arange(N2)
    first = complex_block(2 * math.pi * (np.outer(k1, k1) % N1) / N1)
    second = complex_block(2 * math.pi * (np.outer(k2, k2) % N2) / N2) / 64.0
    second = second.reshape(2, ZH, Q, 8, 2 * N2).transpose(2, 1, 0, 3, 4).reshape(2 * N2, 2 * N2)
    turn = 2 * math.pi * np.outer(k1, k2) / NCH
    first = np.concatenate(halves(first), 0)
    second = np.concatenate(halves(second), 0)
    twiddle = np.stack([np.cos(turn), np.sin(turn)]).astype(np.float32)
    return first, second, twiddle


def channelise_body(core, own, other, hist, taps, first, second, twiddle, out, frames, stage, turned_re, turned_im):
    def place(start, piece):
        for r in range(2):
            frames[r, start : start + piece.shape[1]] = piece[r].astype(F32)

    @pl.when(core[0] == 0)
    def _():
        place(0, hist)
        for s in range(2):
            place(HIST + 2 * SENT * s, own.at[s])
            place(HIST + 2 * SENT * s + SENT, other.at[s])

    @pl.when(core[0] != 0)
    def _():
        for r in range(2):
            frames[r, :3] = own[0, r, 3:].astype(F32)
        for s in range(3):
            place(3 + 2 * SENT * s, other.at[s])
            place(3 + 2 * SENT * s + SENT, own.at[s + 1])

    def pair(step, carry):
        for half in range(2):
            f = 2 * step + half
            for r in range(2):
                acc = taps[0] * frames[r, f]
                for k in range(1, TAPS):
                    acc = acc + taps[k] * frames[r, f + k]
                stage[N1 * r : N1 * (r + 1), N2 * half : N2 * (half + 1)] = acc.astype(BF16)
        both = jnp.dot(first[...], stage[...], preferred_element_type=F32)
        both = both[: 2 * N1] + both[2 * N1 :]
        for half in range(2):
            re = both[:N1, N2 * half : N2 * (half + 1)]
            im = both[N1:, N2 * half : N2 * (half + 1)]
            f = 2 * step + half
            turned_re[pl.ds(f, N1, stride=BLOCK), :] = re * twiddle[0] + im * twiddle[1]
            turned_im[pl.ds(f, N1, stride=BLOCK), :] = im * twiddle[0] - re * twiddle[1]
        return carry

    lax.fori_loop(0, BLOCK // 2, pair, 0)
    for t in range(3):
        rows = slice(256 * t, 256 * (t + 1))
        value = jnp.concatenate([turned_re[rows], turned_im[rows]], 1)
        high = value.astype(BF16)
        low = (value - high.astype(F32)).astype(BF16)
        both = lax.dot_general(second[...], high, NT, preferred_element_type=F32)
        rest = lax.dot_general(second[: 2 * N2], low, NT, preferred_element_type=F32)
        out[:, rows] = (both[: 2 * N2] + (both[2 * N2 :] + rest)).astype(BF16)


def channelise(core, own, other, hist, interpret=False):
    first, second, twiddle = tables()
    args = (core, own, other, hist, prototype(), first, second, twiddle)
    vmem = pl.BlockSpec(memory_space=pltpu.VMEM)
    return pl.pallas_call(
        channelise_body,
        out_shape=jax.ShapeDtypeStruct((2 * N2, N1 * BLOCK), BF16),
        in_specs=[pl.BlockSpec(memory_space=pltpu.SMEM)] + [vmem] * 7,
        out_specs=vmem,
        scratch_shapes=[
            pltpu.VMEM((2, BLOCK + HIST, N1, N2), F32),
            pltpu.VMEM((2 * N1, 2 * N2), BF16),
            pltpu.VMEM((N1 * BLOCK, N2), F32),
            pltpu.VMEM((N1 * BLOCK, N2), F32),
        ],
        compiler_params=PARAMS,
        interpret=interpret,
        name="channelise",
    )(*[jnp.asarray(a) for a in args])


def regroup_body(x, out):
    for z in range(ZH):
        pieces = []
        for c in range(2):
            for r in range(2):
                for i in range(PER):
                    pair = x[2 * i + c, 16 * z : 16 * z + 16, :].astype(F32)
                    pieces.append(pair[8 * r : 8 * r + 8])
        for t in range(N1 * BLOCK // 128):
            piece = jnp.concatenate([p[:, 128 * t : 128 * (t + 1)] for p in pieces], 0).T
            for part in range(16):
                row = 128 * t + 8 * part
                out[row // BLOCK, z, row % BLOCK : row % BLOCK + 8, :] = piece[8 * part : 8 * part + 8].astype(BF16)


def regroup(x, interpret=False):
    vmem = pl.BlockSpec(memory_space=pltpu.VMEM)
    return pl.pallas_call(
        regroup_body,
        out_shape=jax.ShapeDtypeStruct((STN, ZH, BLOCK, 128), BF16),
        in_specs=[vmem],
        out_specs=vmem,
        compiler_params=PARAMS,
        interpret=interpret,
        name="regroup",
    )(x)


def correlate_body(x, out, series, plain):
    most = jnp.zeros((8, 128), F32)
    zero = jnp.zeros((128 - FRAMES, 128), F32)
    for s in range(STN):
        both = jnp.concatenate([x[s, 0].astype(F32), x[s, 1].astype(F32)], 0)
        cols = jnp.concatenate([both, pltpu.roll(both, 64, 1), zero], 0)
        series[64 * s : 64 * (s + 1), :] = cols.T[:64]
    sign = jnp.where(lax.broadcasted_iota(jnp.int32, (STN, 8, 128), 1) < PER, 1.0, -1.0)
    for j in range(8):
        near = series[pl.ds(j, 8 * STN, stride=8), :].reshape(STN, 8, 128)
        far = (pltpu.roll(near, PER, 1) * sign).reshape(8 * STN, 128)
        left = jnp.concatenate([near.reshape(8 * STN, 128), far], 1).astype(BF16)
        right = []
        for r in range(2):
            rows = [series[pl.ds(32 * r + 8 * i + j, STN, stride=64), :] for i in range(PER)]
            right.append(jnp.concatenate(rows, 0))
        right = jnp.concatenate(right, 1).astype(BF16)
        tile = lax.dot_general(left, right, NT, preferred_element_type=F32) / FRAMES
        tile = tile.reshape(STN, 8, 128)
        plain[:, 8 * j : 8 * j + 8, :] = tile
        most = jnp.maximum(most, jnp.max(jnp.abs(tile), 0))
    top = jnp.max(jnp.max(most, 1, keepdims=True), 0, keepdims=True)
    power = jnp.maximum(jnp.floor(jnp.log2(jnp.maximum(top, 1e-37))) - 14.0, -126.0)
    out[:, :64, :] = plain[...] * jnp.exp2(-power).reshape(1, 1, 1)
    out[:, 64:, :] = jnp.broadcast_to(power.reshape(1, 1, 1), (STN, 8, 128))


def correlate(x, interpret=False):
    vmem = pl.BlockSpec(memory_space=pltpu.VMEM)
    return pl.pallas_call(
        correlate_body,
        out_shape=jax.ShapeDtypeStruct((STN, 72, 128), F32),
        in_specs=[vmem],
        out_specs=vmem,
        scratch_shapes=[pltpu.VMEM((64 * STN, 128), F32), pltpu.VMEM((STN, 64, 128), F32)],
        compiler_params=PARAMS,
        interpret=interpret,
        name="correlate",
    )(x)


def deliver_body(x, out, wide, order):
    for k in range(N1):
        wide[64 * k : 64 * (k + 1), :] = x[k, :64, :] * jnp.exp2(x[k, 64:65, :])
    for row in range(8):
        for half in range(2):
            cols = jnp.concatenate(
                [wide[pl.ds(8 * j + row, N1, stride=64), :] for j in range(4 * half, 4 * half + 4)], 0
            ).T
            base = 128 * (2 * row + half)
            for i in range(PER):
                order[pl.ds(base + i, STN, stride=PER), :] = cols[STN * i : STN * (i + 1)]
            out[row // PER, row % PER, :, 128 * half : 128 * (half + 1)] = order[base : base + 128, :]


def deliver(x, interpret=False):
    vmem = pl.BlockSpec(memory_space=pltpu.VMEM)
    return pl.pallas_call(
        deliver_body,
        out_shape=jax.ShapeDtypeStruct((2, PER, 128, 256), F32),
        in_specs=[vmem],
        out_specs=vmem,
        scratch_shapes=[pltpu.VMEM((64 * N1, 128), F32), pltpu.VMEM((16 * 128, 128), F32)],
        compiler_params=PARAMS,
        interpret=interpret,
        name="deliver",
    )(x)


def last_frames(frames):
    q = Q // X * lax.axis_index("x") + lax.axis_index("c")
    rounds = []
    for r in range(X):
        piece = lax.dynamic_index_in_dim(frames, (q + r) % X, 1, False)
        pairs = [(s, Q // X * ((s + r) % X)) for s in range(Q - 3, Q)]
        rounds.append(lax.ppermute(piece, ("zh", "x", "c"), pairs))
    rounds = jnp.stack(rounds)
    parts = [
        lax.dynamic_index_in_dim(rounds, (lax.axis_index("x") - s) % X, 0, False) for s in range(Q - 3, Q)
    ]
    last = jnp.concatenate([parts[0][:, 3:], parts[1], parts[2]], 1)
    return lax.ppermute(last, ("zh", "x", "c"), [(Q // X * x, Q + Q // X * x) for x in range(X)])


def shards(voltages):
    frames = voltages.reshape(2, PER, SENT, N1, N2)
    hist = last_frames(frames)
    core = lax.axis_index("c")
    own = lax.all_to_all(frames.transpose(1, 0, 2, 3, 4), "x", 0, 0, tiled=True)
    other = lax.ppermute(lax.dynamic_slice_in_dim(own, 1 - core, 3, 0), "c", [(0, 1), (1, 0)])
    spectra = channelise(core.astype(jnp.int32).reshape(1), own, other, hist)
    spectra = lax.all_to_all(spectra.reshape(Q, 2 * N2 // Q, N1 * BLOCK), ("x", "c"), 0, 0, tiled=True)
    spectra = regroup(spectra).reshape(STN * ZH, BLOCK, 128)
    spectra = lax.all_to_all(spectra, ("stn", "zh"), 0, 0, tiled=True)
    products = correlate(spectra.reshape(STN, ZH, BLOCK, 128))
    products = lax.all_to_all(products.astype(jnp.float16), "stn", 0, 0, tiled=True)
    return deliver(products.astype(F32))


def solution(mesh):
    split = Mesh(mesh.devices.reshape(STN, ZH, X, Q // X), ("stn", "zh", "x", "c"))
    in_specs = (P(None, "stn", ("zh", "x", "c")),)
    out_specs = P(None, "stn", None, ("zh", "x", "c"))
    return jax.shard_map(shards, mesh=split, in_specs=in_specs, out_specs=out_specs, check_vma=False)
```

```python
import math

import jax
import jax.numpy as jnp
import ml_dtypes
import numpy as np
from jax import lax
from jax.experimental import pallas as pl
from jax.experimental.pallas import tpu as pltpu
from jax.sharding import Mesh
from jax.sharding import PartitionSpec as P

TAPS = 16
NCH = 4096
N1, N2 = 32, 128
STN, ZH, X, Q = 32, 2, 4, 8
FRAMES = 96
BLOCK = 24
HIST = TAPS - 1
SENT = 6
PER = 4
PARAMS = pltpu.CompilerParams(vmem_limit_bytes=48 * 1024 * 1024)
F32, BF16 = jnp.float32, jnp.bfloat16
NT = (((1,), (1,)), ((), ()))


def prototype():
    index = np.arange(TAPS * NCH, dtype=np.float64)
    window = 0.5 - 0.5 * np.cos(2.0 * math.pi * (index + 0.5) / (TAPS * NCH))
    taps = np.sinc((index + 0.5 - TAPS * NCH / 2) / NCH) * window
    return taps.astype(np.float32).reshape(TAPS, N1, N2)


def halves(table):
    high = table.astype(ml_dtypes.bfloat16)
    low = (table - high.astype(np.float64)).astype(ml_dtypes.bfloat16)
    return high, low


def complex_block(angle):
    c, s = np.cos(angle), np.sin(angle)
    return np.block([[c, s], [-s, c]])


def tables():
    k1, k2 = np.arange(N1), np.arange(N2)
    first = complex_block(2 * math.pi * (np.outer(k1, k1) % N1) / N1)
    second = complex_block(2 * math.pi * (np.outer(k2, k2) % N2) / N2) / 64.0
    second = second.reshape(2, ZH, Q, 8, 2 * N2).transpose(2, 1, 0, 3, 4).reshape(2 * N2, 2 * N2)
    turn = 2 * math.pi * np.outer(k1, k2) / NCH
    first = np.concatenate(halves(first), 0)
    second = np.concatenate(halves(second), 0)
    twiddle = np.stack([np.cos(turn), np.sin(turn)]).astype(np.float32)
    return first, second, twiddle


def channelise_body(core, main, hist, taps, first, second, twiddle, out, frames, stage, turned_re, turned_im):
    @pl.when(core[0] == 0)
    def _():
        for r in range(2):
            frames[r, :HIST] = hist[r].astype(F32)
            for s in range(4):
                frames[r, HIST + SENT * s : HIST + SENT * (s + 1)] = main[s, r].astype(F32)

    @pl.when(core[0] != 0)
    def _():
        for r in range(2):
            frames[r, :3] = main[1, r, 3:].astype(F32)
            for s in range(2, 8):
                frames[r, 3 + SENT * (s - 2) : 3 + SENT * (s - 1)] = main[s, r].astype(F32)

    def pair(step, carry):
        for half in range(2):
            f = 2 * step + half
            for r in range(2):
                acc = taps[0] * frames[r, f]
                for k in range(1, TAPS):
                    acc = acc + taps[k] * frames[r, f + k]
                stage[N1 * r : N1 * (r + 1), N2 * half : N2 * (half + 1)] = acc.astype(BF16)
        both = jnp.dot(first[...], stage[...], preferred_element_type=F32)
        both = both[: 2 * N1] + both[2 * N1 :]
        for half in range(2):
            re = both[:N1, N2 * half : N2 * (half + 1)]
            im = both[N1:, N2 * half : N2 * (half + 1)]
            f = 2 * step + half
            turned_re[pl.ds(f, N1, stride=BLOCK), :] = re * twiddle[0] + im * twiddle[1]
            turned_im[pl.ds(f, N1, stride=BLOCK), :] = im * twiddle[0] - re * twiddle[1]
        return carry

    lax.fori_loop(0, BLOCK // 2, pair, 0)
    for t in range(3):
        rows = slice(256 * t, 256 * (t + 1))
        value = jnp.concatenate([turned_re[rows], turned_im[rows]], 1)
        high = value.astype(BF16)
        low = (value - high.astype(F32)).astype(BF16)
        both = lax.dot_general(second[...], high, NT, preferred_element_type=F32)
        rest = lax.dot_general(second[: 2 * N2], low, NT, preferred_element_type=F32)
        out[:, rows] = (both[: 2 * N2] + (both[2 * N2 :] + rest)).astype(BF16)


def channelise(core, main, hist, interpret=False):
    first, second, twiddle = tables()
    args = (core, main, hist, prototype(), first, second, twiddle)
    vmem = pl.BlockSpec(memory_space=pltpu.VMEM)
    return pl.pallas_call(
        channelise_body,
        out_shape=jax.ShapeDtypeStruct((2 * N2, N1 * BLOCK), BF16),
        in_specs=[pl.BlockSpec(memory_space=pltpu.SMEM)] + [vmem] * 6,
        out_specs=vmem,
        scratch_shapes=[
            pltpu.VMEM((2, BLOCK + HIST, N1, N2), F32),
            pltpu.VMEM((2 * N1, 2 * N2), BF16),
            pltpu.VMEM((N1 * BLOCK, N2), F32),
            pltpu.VMEM((N1 * BLOCK, N2), F32),
        ],
        compiler_params=PARAMS,
        interpret=interpret,
        name="channelise",
    )(*[jnp.asarray(a) for a in args])


def regroup_body(x, out):
    for z in range(ZH):
        pieces = []
        for c in range(2):
            for r in range(2):
                for i in range(PER):
                    pair = x[2 * i + c, 16 * z : 16 * z + 16, :].astype(F32)
                    pieces.append(pair[8 * r : 8 * r + 8])
        for t in range(N1 * BLOCK // 128):
            piece = jnp.concatenate([p[:, 128 * t : 128 * (t + 1)] for p in pieces], 0).T
            for part in range(16):
                row = 128 * t + 8 * part
                out[row // BLOCK, z, row % BLOCK : row % BLOCK + 8, :] = piece[8 * part : 8 * part + 8].astype(BF16)


def regroup(x, interpret=False):
    vmem = pl.BlockSpec(memory_space=pltpu.VMEM)
    return pl.pallas_call(
        regroup_body,
        out_shape=jax.ShapeDtypeStruct((STN, ZH, BLOCK, 128), BF16),
        in_specs=[vmem],
        out_specs=vmem,
        compiler_params=PARAMS,
        interpret=interpret,
        name="regroup",
    )(x)


def correlate_body(x, out, series, plain):
    most = jnp.zeros((8, 128), F32)
    zero = jnp.zeros((128 - FRAMES, 128), F32)
    for s in range(STN):
        both = jnp.concatenate([x[s, 0].astype(F32), x[s, 1].astype(F32)], 0)
        cols = jnp.concatenate([both, pltpu.roll(both, 64, 1), zero], 0)
        series[64 * s : 64 * (s + 1), :] = cols.T[:64]
    sign = jnp.where(lax.broadcasted_iota(jnp.int32, (STN, 8, 128), 1) < PER, 1.0, -1.0)
    for j in range(8):
        near = series[pl.ds(j, 8 * STN, stride=8), :].reshape(STN, 8, 128)
        far = (pltpu.roll(near, PER, 1) * sign).reshape(8 * STN, 128)
        left = jnp.concatenate([near.reshape(8 * STN, 128), far], 1).astype(BF16)
        right = []
        for r in range(2):
            rows = [series[pl.ds(32 * r + 8 * i + j, STN, stride=64), :] for i in range(PER)]
            right.append(jnp.concatenate(rows, 0))
        right = jnp.concatenate(right, 1).astype(BF16)
        tile = lax.dot_general(left, right, NT, preferred_element_type=F32) / FRAMES
        tile = tile.reshape(STN, 8, 128)
        plain[:, 8 * j : 8 * j + 8, :] = tile
        most = jnp.maximum(most, jnp.max(jnp.abs(tile), 0))
    top = jnp.max(jnp.max(most, 1, keepdims=True), 0, keepdims=True)
    power = jnp.maximum(jnp.floor(jnp.log2(jnp.maximum(top, 1e-37))) - 14.0, -126.0)
    out[:, :64, :] = plain[...] * jnp.exp2(-power).reshape(1, 1, 1)
    out[:, 64:, :] = jnp.broadcast_to(power.reshape(1, 1, 1), (STN, 8, 128))


def correlate(x, interpret=False):
    vmem = pl.BlockSpec(memory_space=pltpu.VMEM)
    return pl.pallas_call(
        correlate_body,
        out_shape=jax.ShapeDtypeStruct((STN, 72, 128), F32),
        in_specs=[vmem],
        out_specs=vmem,
        scratch_shapes=[pltpu.VMEM((64 * STN, 128), F32), pltpu.VMEM((STN, 64, 128), F32)],
        compiler_params=PARAMS,
        interpret=interpret,
        name="correlate",
    )(x)


def deliver_body(x, out, wide, order):
    for k in range(N1):
        wide[64 * k : 64 * (k + 1), :] = x[k, :64, :] * jnp.exp2(x[k, 64:65, :])
    for row in range(8):
        for half in range(2):
            cols = jnp.concatenate(
                [wide[pl.ds(8 * j + row, N1, stride=64), :] for j in range(4 * half, 4 * half + 4)], 0
            ).T
            base = 128 * (2 * row + half)
            for i in range(PER):
                order[pl.ds(base + i, STN, stride=PER), :] = cols[STN * i : STN * (i + 1)]
            out[row // PER, row % PER, :, 128 * half : 128 * (half + 1)] = order[base : base + 128, :]


def deliver(x, interpret=False):
    vmem = pl.BlockSpec(memory_space=pltpu.VMEM)
    return pl.pallas_call(
        deliver_body,
        out_shape=jax.ShapeDtypeStruct((2, PER, 128, 256), F32),
        in_specs=[vmem],
        out_specs=vmem,
        scratch_shapes=[pltpu.VMEM((64 * N1, 128), F32), pltpu.VMEM((16 * 128, 128), F32)],
        compiler_params=PARAMS,
        interpret=interpret,
        name="deliver",
    )(x)


def last_frames(frames):
    q = Q // X * lax.axis_index("x") + lax.axis_index("c")
    rounds = []
    for r in range(X):
        piece = lax.dynamic_index_in_dim(frames, (q + r) % X, 1, False)
        pairs = [(s, Q // X * ((s + r) % X)) for s in range(Q - 3, Q)]
        rounds.append(lax.ppermute(piece, ("zh", "x", "c"), pairs))
    rounds = jnp.stack(rounds)
    parts = [
        lax.dynamic_index_in_dim(rounds, (lax.axis_index("x") - s) % X, 0, False) for s in range(Q - 3, Q)
    ]
    last = jnp.concatenate([parts[0][:, 3:], parts[1], parts[2]], 1)
    return lax.ppermute(last, ("zh", "x", "c"), [(Q // X * x, Q + Q // X * x) for x in range(X)])


def shards(voltages):
    frames = voltages.reshape(2, PER, SENT, N1, N2)
    hist = last_frames(frames)
    doubled = jnp.repeat(frames.transpose(1, 0, 2, 3, 4), Q // X, 0)
    half = lax.all_to_all(doubled, ("x", "c"), 0, 0, tiled=True)
    core = lax.axis_index("c").astype(jnp.int32).reshape(1)
    spectra = channelise(core, half, hist)
    spectra = lax.all_to_all(spectra.reshape(Q, 2 * N2 // Q, N1 * BLOCK), ("x", "c"), 0, 0, tiled=True)
    spectra = regroup(spectra).reshape(STN * ZH, BLOCK, 128)
    spectra = lax.all_to_all(spectra, ("stn", "zh"), 0, 0, tiled=True)
    products = correlate(spectra.reshape(STN, ZH, BLOCK, 128))
    products = lax.all_to_all(products.astype(jnp.float16), "stn", 0, 0, tiled=True)
    return deliver(products.astype(F32))


def solution(mesh):
    split = Mesh(mesh.devices.reshape(STN, ZH, X, Q // X), ("stn", "zh", "x", "c"))
    in_specs = (P(None, "stn", ("zh", "x", "c")),)
    out_specs = P(None, "stn", None, ("zh", "x", "c"))
    return jax.shard_map(shards, mesh=split, in_specs=in_specs, out_specs=out_specs, check_vma=False)
```

```python
import math

import jax
import jax.numpy as jnp
import ml_dtypes
import numpy as np
from jax import lax
from jax.experimental import pallas as pl
from jax.experimental.pallas import tpu as pltpu
from jax.sharding import Mesh
from jax.sharding import PartitionSpec as P

TAPS = 16
NCH = 4096
N1, N2 = 32, 128
STN, ZH, X, Q = 32, 2, 4, 8
FRAMES = 96
BLOCK = 24
HIST = TAPS - 1
SENT = 6
PER = 4
PARAMS = pltpu.CompilerParams(vmem_limit_bytes=48 * 1024 * 1024)
F32, BF16 = jnp.float32, jnp.bfloat16
NT = (((1,), (1,)), ((), ()))


def prototype():
    index = np.arange(TAPS * NCH, dtype=np.float64)
    window = 0.5 - 0.5 * np.cos(2.0 * math.pi * (index + 0.5) / (TAPS * NCH))
    taps = np.sinc((index + 0.5 - TAPS * NCH / 2) / NCH) * window
    return taps.astype(np.float32).reshape(TAPS, N1, N2)


def halves(table):
    high = table.astype(ml_dtypes.bfloat16)
    low = (table - high.astype(np.float64)).astype(ml_dtypes.bfloat16)
    return high, low


def complex_block(angle):
    c, s = np.cos(angle), np.sin(angle)
    return np.block([[c, s], [-s, c]])


def tables():
    k1, k2 = np.arange(N1), np.arange(N2)
    first = complex_block(2 * math.pi * (np.outer(k1, k1) % N1) / N1)
    second = complex_block(2 * math.pi * (np.outer(k2, k2) % N2) / N2) / 64.0
    second = second.reshape(2, ZH, Q, 8, 2 * N2).transpose(2, 1, 0, 3, 4).reshape(2 * N2, 2 * N2)
    turn = 2 * math.pi * np.outer(k1, k2) / NCH
    first = np.concatenate(halves(first), 0)
    second = np.concatenate(halves(second), 0)
    twiddle = np.stack([np.cos(turn), np.sin(turn)]).astype(np.float32)
    return first, second, twiddle


def channelise_body(place, main, hist, taps, first, second, twiddle, out, frames, stage, turned_re, turned_im):
    @pl.when(place[0] == 0)
    def _():
        for r in range(2):
            frames[r, :HIST] = hist[r].astype(F32)
            for s in range(4):
                frames[r, HIST + SENT * s : HIST + SENT * (s + 1)] = main[s, r].astype(F32)

    @pl.when(place[0] != 0)
    def _():
        for r in range(2):
            frames[r, :3] = main[1, r, 3:].astype(F32)
            for s in range(2, 8):
                frames[r, 3 + SENT * (s - 2) : 3 + SENT * (s - 1)] = main[s, r].astype(F32)

    def pair(step, carry):
        for t in range(0, N1, 16):
            rows = slice(t, t + 16)
            for r in range(2):
                early = frames[r, 2 * step, rows]
                sums = None
                for k in range(TAPS):
                    late = frames[r, 2 * step + k + 1, rows]
                    tap = taps[k, rows]
                    terms = (tap * early, tap * late)
                    sums = terms if sums is None else (sums[0] + terms[0], sums[1] + terms[1])
                    early = late
                for half in range(2):
                    stage[N1 * r + t : N1 * r + t + 16, N2 * half : N2 * (half + 1)] = sums[half].astype(BF16)
        both = jnp.dot(first[...], stage[...], preferred_element_type=F32)
        both = both[: 2 * N1] + both[2 * N1 :]
        for half in range(2):
            re = both[:N1, N2 * half : N2 * (half + 1)]
            im = both[N1:, N2 * half : N2 * (half + 1)]
            f = 2 * step + half
            turned_re[pl.ds(f, N1, stride=BLOCK), :] = re * twiddle[0] + im * twiddle[1]
            turned_im[pl.ds(f, N1, stride=BLOCK), :] = im * twiddle[0] - re * twiddle[1]
        return carry

    lax.fori_loop(0, BLOCK // 2, pair, 0)
    for t in range(3):
        rows = slice(256 * t, 256 * (t + 1))
        value = jnp.concatenate([turned_re[rows], turned_im[rows]], 1)
        high = value.astype(BF16)
        low = (value - high.astype(F32)).astype(BF16)
        both = lax.dot_general(second[...], high, NT, preferred_element_type=F32)
        rest = lax.dot_general(second[: 2 * N2], low, NT, preferred_element_type=F32)
        out[:, rows] = (both[: 2 * N2] + (both[2 * N2 :] + rest)).astype(BF16)


def channelise(place, main, hist, interpret=False):
    first, second, twiddle = tables()
    args = (place, main, hist, prototype(), first, second, twiddle)
    vmem = pl.BlockSpec(memory_space=pltpu.VMEM)
    return pl.pallas_call(
        channelise_body,
        out_shape=jax.ShapeDtypeStruct((2 * N2, N1 * BLOCK), BF16),
        in_specs=[pl.BlockSpec(memory_space=pltpu.SMEM)] + [vmem] * 6,
        out_specs=vmem,
        scratch_shapes=[
            pltpu.VMEM((2, BLOCK + HIST, N1, N2), F32),
            pltpu.VMEM((2 * N1, 2 * N2), BF16),
            pltpu.VMEM((N1 * BLOCK, N2), F32),
            pltpu.VMEM((N1 * BLOCK, N2), F32),
        ],
        compiler_params=PARAMS,
        interpret=interpret,
        name="channelise",
    )(*[jnp.asarray(a) for a in args])


def regroup_body(x, out):
    for z in range(ZH):
        pieces = []
        for c in range(2):
            for r in range(2):
                for i in range(PER):
                    pair = x[2 * i + c, 16 * z : 16 * z + 16, :].astype(F32)
                    pieces.append(pair[8 * r : 8 * r + 8])
        for t in range(N1 * BLOCK // 128):
            piece = jnp.concatenate([p[:, 128 * t : 128 * (t + 1)] for p in pieces], 0).T
            for part in range(16):
                row = 128 * t + 8 * part
                out[row // BLOCK, z, row % BLOCK : row % BLOCK + 8, :] = piece[8 * part : 8 * part + 8].astype(BF16)


def regroup(x, interpret=False):
    vmem = pl.BlockSpec(memory_space=pltpu.VMEM)
    return pl.pallas_call(
        regroup_body,
        out_shape=jax.ShapeDtypeStruct((STN, ZH, BLOCK, 128), BF16),
        in_specs=[vmem],
        out_specs=vmem,
        compiler_params=PARAMS,
        interpret=interpret,
        name="regroup",
    )(x)


def correlate_body(x, out, series, plain):
    most = jnp.zeros((8, 128), F32)
    zero = jnp.zeros((128 - FRAMES, 128), F32)
    for s in range(STN):
        both = jnp.concatenate([x[s, 0].astype(F32), x[s, 1].astype(F32)], 0)
        cols = jnp.concatenate([both, pltpu.roll(both, 64, 1), zero], 0)
        series[64 * s : 64 * (s + 1), :] = cols.T[:64]
    sign = jnp.where(lax.broadcasted_iota(jnp.int32, (STN, 8, 128), 1) < PER, 1.0, -1.0)
    for j in range(8):
        near = series[pl.ds(j, 8 * STN, stride=8), :].reshape(STN, 8, 128)
        far = (pltpu.roll(near, PER, 1) * sign).reshape(8 * STN, 128)
        left = jnp.concatenate([near.reshape(8 * STN, 128), far], 1).astype(BF16)
        right = []
        for r in range(2):
            rows = [series[pl.ds(32 * r + 8 * i + j, STN, stride=64), :] for i in range(PER)]
            right.append(jnp.concatenate(rows, 0))
        right = jnp.concatenate(right, 1).astype(BF16)
        tile = lax.dot_general(left, right, NT, preferred_element_type=F32) / FRAMES
        tile = tile.reshape(STN, 8, 128)
        plain[:, 8 * j : 8 * j + 8, :] = tile
        most = jnp.maximum(most, jnp.max(jnp.abs(tile), 0))
    top = jnp.max(jnp.max(most, 1, keepdims=True), 0, keepdims=True)
    power = jnp.maximum(jnp.floor(jnp.log2(jnp.maximum(top, 1e-37))) - 14.0, -126.0)
    factor, power = jnp.exp2(-power).reshape(1, 1, 1), power.reshape(1, 1, 1)
    station, row, lane = (lax.broadcasted_iota(jnp.int32, (STN, 8, 128), d) for d in range(3))
    out[:, :8, :] = jnp.where((row == 1) & (lane == station), power, plain[:, :8, :] * factor)
    out[:, 8:, :] = plain[:, 8:, :] * factor


def correlate(x, interpret=False):
    vmem = pl.BlockSpec(memory_space=pltpu.VMEM)
    return pl.pallas_call(
        correlate_body,
        out_shape=jax.ShapeDtypeStruct((STN, 64, 128), F32),
        in_specs=[vmem],
        out_specs=vmem,
        scratch_shapes=[pltpu.VMEM((64 * STN, 128), F32), pltpu.VMEM((STN, 64, 128), F32)],
        compiler_params=PARAMS,
        interpret=interpret,
        name="correlate",
    )(x)


def deliver_body(place, x, out, wide, order):
    row = pl.program_id(0)

    @pl.when(row == 0)
    def _():
        here = x[:, :8, :]
        line, lane = (lax.broadcasted_iota(jnp.int32, (N1, 8, 128), d) for d in (1, 2))
        holder = (line == 1) & (lane == place[1])
        mirror = (line == 0) & (lane == place[1] + STN)

        def pick(mask):
            return jnp.sum(jnp.sum(jnp.where(mask, here, 0.0), 2, keepdims=True), 1, keepdims=True)

        factor = jnp.exp2(pick(holder))
        wide[:, :8, :] = jnp.where(holder, pick(mirror), here) * factor
        wide[:, 8:, :] = x[:, 8:, :] * factor

    flat = wide.reshape(64 * N1, 128)
    for half in range(2):
        rows = [flat[pl.ds(8 * j + row, N1, stride=64), :] for j in range(4 * half, 4 * half + 4)]
        cols = jnp.concatenate(rows, 0).T
        for i in range(PER):
            order[pl.ds(128 * half + i, STN, stride=PER), :] = cols[STN * i : STN * (i + 1)]
        out[0, 0, :, 128 * half : 128 * (half + 1)] = order[128 * half : 128 * (half + 1), :]


def deliver(place, x, interpret=False):
    return pl.pallas_call(
        deliver_body,
        grid=(8,),
        out_shape=jax.ShapeDtypeStruct((2, PER, 128, 256), F32),
        in_specs=[pl.BlockSpec(memory_space=pltpu.SMEM), pl.BlockSpec(memory_space=pltpu.VMEM)],
        out_specs=pl.BlockSpec((1, 1, 128, 256), lambda row: (row // PER, row % PER, 0, 0)),
        scratch_shapes=[pltpu.VMEM((N1, 64, 128), F32), pltpu.VMEM((2 * 128, 128), F32)],
        compiler_params=PARAMS,
        interpret=interpret,
        name="deliver",
    )(place, x)


def last_frames(frames):
    q = Q // X * lax.axis_index("x") + lax.axis_index("c")
    rounds = []
    for r in range(X):
        piece = lax.dynamic_index_in_dim(frames, (q + r) % X, 1, False)
        pairs = [(s, Q // X * ((s + r) % X)) for s in range(Q - 3, Q)]
        rounds.append(lax.ppermute(piece, ("zh", "x", "c"), pairs))
    rounds = jnp.stack(rounds)
    parts = [
        lax.dynamic_index_in_dim(rounds, (lax.axis_index("x") - s) % X, 0, False) for s in range(Q - 3, Q)
    ]
    last = jnp.concatenate([parts[0][:, 3:], parts[1], parts[2]], 1)
    return lax.ppermute(last, ("zh", "x", "c"), [(Q // X * x, Q + Q // X * x) for x in range(X)])


def shards(voltages):
    frames = voltages.reshape(2, PER, SENT, N1, N2)
    hist = last_frames(frames)
    doubled = jnp.repeat(frames.transpose(1, 0, 2, 3, 4), Q // X, 0)
    half = lax.all_to_all(doubled, ("x", "c"), 0, 0, tiled=True)
    place = jnp.stack([lax.axis_index("c"), lax.axis_index("stn")]).astype(jnp.int32)
    spectra = channelise(place, half, hist)
    spectra = lax.all_to_all(spectra.reshape(Q, 2 * N2 // Q, N1 * BLOCK), ("x", "c"), 0, 0, tiled=True)
    spectra = regroup(spectra).reshape(STN * ZH, BLOCK, 128)
    spectra = lax.all_to_all(spectra, ("stn", "zh"), 0, 0, tiled=True)
    products = correlate(spectra.reshape(STN, ZH, BLOCK, 128))
    products = lax.all_to_all(products.astype(jnp.float16), "stn", 0, 0, tiled=True)
    return deliver(place, products.astype(F32))


def solution(mesh):
    split = Mesh(mesh.devices.reshape(STN, ZH, X, Q // X), ("stn", "zh", "x", "c"))
    in_specs = (P(None, "stn", ("zh", "x", "c")),)
    out_specs = P(None, "stn", None, ("zh", "x", "c"))
    return jax.shard_map(shards, mesh=split, in_specs=in_specs, out_specs=out_specs, check_vma=False)
```

```python
import math

import jax
import jax.numpy as jnp
import ml_dtypes
import numpy as np
from jax import lax
from jax.experimental import pallas as pl
from jax.experimental.pallas import tpu as pltpu
from jax.sharding import Mesh
from jax.sharding import PartitionSpec as P

TAPS = 16
NCH = 4096
N1, N2 = 32, 128
STN, ZH, X, Q = 32, 2, 4, 8
FRAMES = 96
BLOCK = 24
HIST = TAPS - 1
SENT = 6
PER = 4
PARAMS = pltpu.CompilerParams(vmem_limit_bytes=48 * 1024 * 1024)
F32, BF16 = jnp.float32, jnp.bfloat16
NT = (((1,), (1,)), ((), ()))


def prototype():
    index = np.arange(TAPS * NCH, dtype=np.float64)
    window = 0.5 - 0.5 * np.cos(2.0 * math.pi * (index + 0.5) / (TAPS * NCH))
    taps = np.sinc((index + 0.5 - TAPS * NCH / 2) / NCH) * window
    return taps.astype(np.float32).reshape(TAPS, N1, N2)


def halves(table):
    high = table.astype(ml_dtypes.bfloat16)
    low = (table - high.astype(np.float64)).astype(ml_dtypes.bfloat16)
    return high, low


def complex_block(angle):
    c, s = np.cos(angle), np.sin(angle)
    return np.block([[c, s], [-s, c]])


def tables():
    k1, k2 = np.arange(N1), np.arange(N2)
    first = complex_block(2 * math.pi * (np.outer(k1, k1) % N1) / N1)
    second = complex_block(2 * math.pi * (np.outer(k2, k2) % N2) / N2) / 64.0
    second = second.reshape(2, ZH, Q, 8, 2 * N2).transpose(2, 1, 0, 3, 4).reshape(2 * N2, 2 * N2)
    turn = 2 * math.pi * np.outer(k1, k2) / NCH
    first = np.concatenate(halves(first), 0)
    second = np.concatenate(halves(second), 0)
    twiddle = np.stack([np.cos(turn), np.sin(turn)]).astype(np.float32)
    return first, second, twiddle


def channelise_body(place, main, hist, taps, first, second, twiddle, out, frames, stage, turned_re, turned_im):
    @pl.when(place[0] == 0)
    def _():
        for r in range(2):
            frames[r, :HIST] = hist[r].astype(F32)
            for s in range(4):
                frames[r, HIST + SENT * s : HIST + SENT * (s + 1)] = main[s, r].astype(F32)

    @pl.when(place[0] != 0)
    def _():
        for r in range(2):
            frames[r, :3] = main[1, r, 3:].astype(F32)
            for s in range(2, 8):
                frames[r, 3 + SENT * (s - 2) : 3 + SENT * (s - 1)] = main[s, r].astype(F32)

    def pair(step, carry):
        for half in range(2):
            f = 2 * step + half
            for r in range(2):
                acc = taps[0] * frames[r, f]
                for k in range(1, TAPS):
                    acc = acc + taps[k] * frames[r, f + k]
                stage[N1 * r : N1 * (r + 1), N2 * half : N2 * (half + 1)] = acc.astype(BF16)
        both = jnp.dot(first[...], stage[...], preferred_element_type=F32)
        both = both[: 2 * N1] + both[2 * N1 :]
        for half in range(2):
            re = both[:N1, N2 * half : N2 * (half + 1)]
            im = both[N1:, N2 * half : N2 * (half + 1)]
            f = 2 * step + half
            turned_re[pl.ds(f, N1, stride=BLOCK), :] = re * twiddle[0] + im * twiddle[1]
            turned_im[pl.ds(f, N1, stride=BLOCK), :] = im * twiddle[0] - re * twiddle[1]
        return carry

    lax.fori_loop(0, BLOCK // 2, pair, 0)
    for t in range(3):
        rows = slice(256 * t, 256 * (t + 1))
        value = jnp.concatenate([turned_re[rows], turned_im[rows]], 1)
        high = value.astype(BF16)
        low = (value - high.astype(F32)).astype(BF16)
        both = lax.dot_general(second[...], high, NT, preferred_element_type=F32)
        rest = lax.dot_general(second[: 2 * N2], low, NT, preferred_element_type=F32)
        out[:, rows] = (both[: 2 * N2] + (both[2 * N2 :] + rest)).astype(BF16)


def channelise(place, main, hist, interpret=False):
    first, second, twiddle = tables()
    args = (place, main, hist, prototype(), first, second, twiddle)
    vmem = pl.BlockSpec(memory_space=pltpu.VMEM)
    return pl.pallas_call(
        channelise_body,
        out_shape=jax.ShapeDtypeStruct((2 * N2, N1 * BLOCK), BF16),
        in_specs=[pl.BlockSpec(memory_space=pltpu.SMEM)] + [vmem] * 6,
        out_specs=vmem,
        scratch_shapes=[
            pltpu.VMEM((2, BLOCK + HIST, N1, N2), F32),
            pltpu.VMEM((2 * N1, 2 * N2), BF16),
            pltpu.VMEM((N1 * BLOCK, N2), F32),
            pltpu.VMEM((N1 * BLOCK, N2), F32),
        ],
        compiler_params=PARAMS,
        interpret=interpret,
        name="channelise",
    )(*[jnp.asarray(a) for a in args])


def regroup_body(x, out):
    for z in range(ZH):
        pieces = []
        for c in range(2):
            for r in range(2):
                for i in range(PER):
                    pair = x[2 * i + c, 16 * z : 16 * z + 16, :].astype(F32)
                    pieces.append(pair[8 * r : 8 * r + 8])
        for t in range(N1 * BLOCK // 128):
            piece = jnp.concatenate([p[:, 128 * t : 128 * (t + 1)] for p in pieces], 0).T
            for part in range(16):
                row = 128 * t + 8 * part
                out[row // BLOCK, z, row % BLOCK : row % BLOCK + 8, :] = piece[8 * part : 8 * part + 8].astype(BF16)


def regroup(x, interpret=False):
    vmem = pl.BlockSpec(memory_space=pltpu.VMEM)
    return pl.pallas_call(
        regroup_body,
        out_shape=jax.ShapeDtypeStruct((STN, ZH, BLOCK, 128), BF16),
        in_specs=[vmem],
        out_specs=vmem,
        compiler_params=PARAMS,
        interpret=interpret,
        name="regroup",
    )(x)


def correlate_body(x, out, series, plain):
    most = jnp.zeros((8, 128), F32)
    zero = jnp.zeros((128 - FRAMES, 128), F32)
    for s in range(STN):
        both = jnp.concatenate([x[s, 0].astype(F32), x[s, 1].astype(F32)], 0)
        cols = jnp.concatenate([both, pltpu.roll(both, 64, 1), zero], 0)
        series[64 * s : 64 * (s + 1), :] = cols.T[:64]
    sign = jnp.where(lax.broadcasted_iota(jnp.int32, (STN, 8, 128), 1) < PER, 1.0, -1.0)
    for j in range(8):
        near = series[pl.ds(j, 8 * STN, stride=8), :].reshape(STN, 8, 128)
        far = (pltpu.roll(near, PER, 1) * sign).reshape(8 * STN, 128)
        left = jnp.concatenate([near.reshape(8 * STN, 128), far], 1).astype(BF16)
        right = []
        for r in range(2):
            rows = [series[pl.ds(32 * r + 8 * i + j, STN, stride=64), :] for i in range(PER)]
            right.append(jnp.concatenate(rows, 0))
        right = jnp.concatenate(right, 1).astype(BF16)
        tile = lax.dot_general(left, right, NT, preferred_element_type=F32) / FRAMES
        tile = tile.reshape(STN, 8, 128)
        plain[:, 8 * j : 8 * j + 8, :] = tile
        most = jnp.maximum(most, jnp.max(jnp.abs(tile), 0))
    top = jnp.max(jnp.max(most, 1, keepdims=True), 0, keepdims=True)
    power = jnp.maximum(jnp.floor(jnp.log2(jnp.maximum(top, 1e-37))) - 14.0, -126.0)
    factor, power = jnp.exp2(-power).reshape(1, 1, 1), power.reshape(1, 1, 1)
    station, row, lane = (lax.broadcasted_iota(jnp.int32, (STN, 8, 128), d) for d in range(3))
    out[:, :8, :] = jnp.where((row == 1) & (lane == station), power, plain[:, :8, :] * factor)
    out[:, 8:, :] = plain[:, 8:, :] * factor


def correlate(x, interpret=False):
    vmem = pl.BlockSpec(memory_space=pltpu.VMEM)
    return pl.pallas_call(
        correlate_body,
        out_shape=jax.ShapeDtypeStruct((STN, 64, 128), F32),
        in_specs=[vmem],
        out_specs=vmem,
        scratch_shapes=[pltpu.VMEM((64 * STN, 128), F32), pltpu.VMEM((STN, 64, 128), F32)],
        compiler_params=PARAMS,
        interpret=interpret,
        name="correlate",
    )(x)


def deliver_body(place, x, out, wide, order):
    here = x[:, :8, :]
    line, lane = (lax.broadcasted_iota(jnp.int32, (N1, 8, 128), d) for d in (1, 2))
    holder = (line == 1) & (lane == place[1])
    mirror = (line == 0) & (lane == place[1] + STN)

    def pick(mask):
        return jnp.sum(jnp.sum(jnp.where(mask, here, 0.0), 1, keepdims=True), 2, keepdims=True)

    factor = jnp.exp2(pick(holder))
    wide[...] = x[...] * factor
    wide[:, :8, :] = jnp.where(holder, pick(mirror), here) * factor
    flat = wide.reshape(64 * N1, 128)
    for row in range(8):
        for half in range(2):
            rows = [flat[pl.ds(8 * j + row, N1, stride=64), :] for j in range(4 * half, 4 * half + 4)]
            cols = jnp.concatenate(rows, 0).T
            base = 128 * (2 * row + half)
            for i in range(PER):
                order[pl.ds(base + i, STN, stride=PER), :] = cols[STN * i : STN * (i + 1)]
            out[row // PER, row % PER, :, 128 * half : 128 * (half + 1)] = order[base : base + 128, :]


def deliver(place, x, interpret=False):
    vmem = pl.BlockSpec(memory_space=pltpu.VMEM)
    return pl.pallas_call(
        deliver_body,
        out_shape=jax.ShapeDtypeStruct((2, PER, 128, 256), F32),
        in_specs=[pl.BlockSpec(memory_space=pltpu.SMEM), vmem],
        out_specs=vmem,
        scratch_shapes=[pltpu.VMEM((N1, 64, 128), F32), pltpu.VMEM((16 * 128, 128), F32)],
        compiler_params=PARAMS,
        interpret=interpret,
        name="deliver",
    )(place, x)


def last_frames(frames):
    q = Q // X * lax.axis_index("x") + lax.axis_index("c")
    rounds = []
    for r in range(X):
        piece = lax.dynamic_index_in_dim(frames, (q + r) % X, 1, False)
        pairs = [(s, Q // X * ((s + r) % X)) for s in range(Q - 3, Q)]
        rounds.append(lax.ppermute(piece, ("zh", "x", "c"), pairs))
    rounds = jnp.stack(rounds)
    parts = [
        lax.dynamic_index_in_dim(rounds, (lax.axis_index("x") - s) % X, 0, False) for s in range(Q - 3, Q)
    ]
    last = jnp.concatenate([parts[0][:, 3:], parts[1], parts[2]], 1)
    return lax.ppermute(last, ("zh", "x", "c"), [(Q // X * x, Q + Q // X * x) for x in range(X)])


def shards(voltages):
    frames = voltages.reshape(2, PER, SENT, N1, N2)
    hist = last_frames(frames)
    doubled = jnp.repeat(frames.transpose(1, 0, 2, 3, 4), Q // X, 0)
    half = lax.all_to_all(doubled, ("x", "c"), 0, 0, tiled=True)
    place = jnp.stack([lax.axis_index("c"), lax.axis_index("stn")]).astype(jnp.int32)
    spectra = channelise(place, half, hist)
    spectra = lax.all_to_all(spectra.reshape(Q, 2 * N2 // Q, N1 * BLOCK), ("x", "c"), 0, 0, tiled=True)
    spectra = regroup(spectra).reshape(STN * ZH, BLOCK, 128)
    spectra = lax.all_to_all(spectra, ("stn", "zh"), 0, 0, tiled=True)
    products = correlate(spectra.reshape(STN, ZH, BLOCK, 128))
    products = lax.all_to_all(products.astype(jnp.float16), "stn", 0, 0, tiled=True)
    return deliver(place, products.astype(F32))


def solution(mesh):
    split = Mesh(mesh.devices.reshape(STN, ZH, X, Q // X), ("stn", "zh", "x", "c"))
    in_specs = (P(None, "stn", ("zh", "x", "c")),)
    out_specs = P(None, "stn", None, ("zh", "x", "c"))
    return jax.shard_map(shards, mesh=split, in_specs=in_specs, out_specs=out_specs, check_vma=False)
```

```python
import math

import jax
import jax.numpy as jnp
import ml_dtypes
import numpy as np
from jax import lax
from jax.experimental import pallas as pl
from jax.experimental.pallas import tpu as pltpu
from jax.sharding import Mesh
from jax.sharding import PartitionSpec as P

TAPS = 16
NCH = 4096
N1, N2 = 32, 128
STN, ZH, X, Q = 32, 2, 4, 8
FRAMES = 96
BLOCK = 24
HIST = TAPS - 1
LATE = 8
FEW = BLOCK - LATE
SENT = 6
PER = 4
PARAMS = pltpu.CompilerParams(vmem_limit_bytes=48 * 1024 * 1024)
F32, BF16 = jnp.float32, jnp.bfloat16
NT = (((1,), (1,)), ((), ()))


def prototype():
    index = np.arange(TAPS * NCH, dtype=np.float64)
    window = 0.5 - 0.5 * np.cos(2.0 * math.pi * (index + 0.5) / (TAPS * NCH))
    taps = np.sinc((index + 0.5 - TAPS * NCH / 2) / NCH) * window
    return taps.astype(np.float32).reshape(TAPS, N1, N2)


def halves(table):
    high = table.astype(ml_dtypes.bfloat16)
    low = (table - high.astype(np.float64)).astype(ml_dtypes.bfloat16)
    return high, low


def complex_block(angle):
    c, s = np.cos(angle), np.sin(angle)
    return np.block([[c, s], [-s, c]])


def tables():
    k1, k2 = np.arange(N1), np.arange(N2)
    first = complex_block(2 * math.pi * (np.outer(k1, k1) % N1) / N1)
    second = complex_block(2 * math.pi * (np.outer(k2, k2) % N2) / N2) / 64.0
    second = second.reshape(2, ZH, Q, 8, 2 * N2).transpose(2, 1, 0, 3, 4).reshape(2 * N2, 2 * N2)
    turn = 2 * math.pi * np.outer(k1, k2) / NCH
    first = np.concatenate(halves(first), 0)
    second = np.concatenate(halves(second), 0)
    twiddle = np.stack([np.cos(turn), np.sin(turn)]).astype(np.float32)
    return first, second, twiddle


def spectrum(filtered, count, first, second, twiddle, stage, turned_re, turned_im, out):
    def pair(step, carry):
        for half in range(2):
            for r in range(2):
                stage[N1 * r : N1 * (r + 1), N2 * half : N2 * (half + 1)] = filtered(r, 2 * step + half).astype(BF16)
        both = jnp.dot(first[...], stage[...], preferred_element_type=F32)
        both = both[: 2 * N1] + both[2 * N1 :]
        for half in range(2):
            re = both[:N1, N2 * half : N2 * (half + 1)]
            im = both[N1:, N2 * half : N2 * (half + 1)]
            rows = pl.ds(2 * step + half, N1, stride=count)
            turned_re[rows, :] = re * twiddle[0] + im * twiddle[1]
            turned_im[rows, :] = im * twiddle[0] - re * twiddle[1]
        return carry

    lax.fori_loop(0, count // 2, pair, 0)
    for t in range(N1 * count // 256):
        rows = slice(256 * t, 256 * (t + 1))
        value = jnp.concatenate([turned_re[rows], turned_im[rows]], 1)
        high = value.astype(BF16)
        low = (value - high.astype(F32)).astype(BF16)
        both = lax.dot_general(second[...], high, NT, preferred_element_type=F32)
        rest = lax.dot_general(second[: 2 * N2], low, NT, preferred_element_type=F32)
        out[:, rows] = (both[: 2 * N2] + (both[2 * N2 :] + rest)).astype(BF16)


def early_body(core, station, main, taps, first, second, twiddle, sums, out, frames, stage, turned_re, turned_im):
    @pl.when(core[0] == 0)
    def _():
        for r in range(2):
            frames[r, :HIST] = jnp.zeros((HIST, N1, N2), F32)
            for s in range(4):
                frames[r, HIST + SENT * s : HIST + SENT * (s + 1)] = main[s, r].astype(F32)

    @pl.when(core[0] != 0)
    def _():
        for r in range(2):
            frames[r, :3] = main[1, r, 3:].astype(F32)
            for s in range(2, 8):
                frames[r, 3 + SENT * (s - 2) : 3 + SENT * (s - 1)] = main[s, r].astype(F32)

    def filtered(r, f):
        acc = taps[0] * frames[r, f]
        for k in range(1, TAPS):
            acc = acc + taps[k] * frames[r, f + k]
        return acc

    def keep(f, carry):
        for r in range(2):
            sums[r, f] = filtered(r, f)
        return carry

    lax.fori_loop(0, FEW, keep, 0)
    late = lambda r, f: filtered(r, FEW + f)
    spectrum(late, LATE, first, second, twiddle, stage, turned_re, turned_im, out)


def rest_body(core, station, sums, hist, done, taps, first, second, twiddle, out, total, past, stage, turned_re, turned_im):
    out[:, N1 * FEW :] = done[...]
    total[...] = sums[...]

    @pl.when(core[0] == 0)
    def _():
        past[...] = hist[...].astype(F32)
        for f in range(HIST):
            for r in range(2):
                acc = sums[r, f]
                for k in range(HIST - f):
                    acc = acc + taps[k] * past[r, f + k]
                total[r, f] = acc

    spectrum(lambda r, f: total[r, f], FEW, first, second, twiddle, stage, turned_re, turned_im, out)


def kernel(body, scalars, args, out_shape, scratch, frames, name, interpret):
    vmem = pl.BlockSpec(memory_space=pltpu.VMEM)
    scratch = scratch + [
        pltpu.VMEM((2 * N1, 2 * N2), BF16),
        pltpu.VMEM((N1 * frames, N2), F32),
        pltpu.VMEM((N1 * frames, N2), F32),
    ]
    return pl.pallas_call(
        body,
        out_shape=out_shape,
        in_specs=[pl.BlockSpec(memory_space=pltpu.SMEM)] * len(scalars) + [vmem] * len(args),
        out_specs=jax.tree.map(lambda _: vmem, out_shape),
        scratch_shapes=scratch,
        compiler_params=PARAMS,
        interpret=interpret,
        name=name,
    )(*scalars, *args)


def channelise(scalars, main, hist, interpret=False):
    fixed = [jnp.asarray(a) for a in (prototype(), *tables())]
    shape = jax.ShapeDtypeStruct
    outs = (shape((2, FEW, N1, N2), F32), shape((2 * N2, N1 * LATE), BF16))
    scratch = [pltpu.VMEM((2, BLOCK + HIST, N1, N2), F32)]
    sums, done = kernel(early_body, scalars, (main, *fixed), outs, scratch, LATE, "early", interpret)
    outs = shape((2 * N2, N1 * BLOCK), BF16)
    scratch = [pltpu.VMEM((2, FEW, N1, N2), F32), pltpu.VMEM((2, HIST, N1, N2), F32)]
    return kernel(rest_body, scalars, (sums, hist, done, *fixed), outs, scratch, FEW, "rest", interpret)


def regroup_body(x, out):
    for z in range(ZH):
        pieces = []
        for c in range(2):
            for r in range(2):
                for i in range(PER):
                    pair = x[2 * i + c, 16 * z : 16 * z + 16, :].astype(F32)
                    pieces.append(pair[8 * r : 8 * r + 8])
        for t in range(N1 * BLOCK // 128):
            piece = jnp.concatenate([p[:, 128 * t : 128 * (t + 1)] for p in pieces], 0).T
            for part in range(16):
                k, f = divmod(128 * t + 8 * part, FEW)
                if k >= N1:
                    k, f = 16 * t + part - N1 * FEW // 8, FEW
                out[k, z, f : f + 8, :] = piece[8 * part : 8 * part + 8].astype(BF16)


def regroup(x, interpret=False):
    vmem = pl.BlockSpec(memory_space=pltpu.VMEM)
    return pl.pallas_call(
        regroup_body,
        out_shape=jax.ShapeDtypeStruct((STN, ZH, BLOCK, 128), BF16),
        in_specs=[vmem],
        out_specs=vmem,
        compiler_params=PARAMS,
        interpret=interpret,
        name="regroup",
    )(x)


def correlate_body(x, out, series, plain):
    most = jnp.zeros((8, 128), F32)
    zero = jnp.zeros((128 - FRAMES, 128), F32)
    for s in range(STN):
        both = jnp.concatenate([x[s, 0].astype(F32), x[s, 1].astype(F32)], 0)
        cols = jnp.concatenate([both, pltpu.roll(both, 64, 1), zero], 0)
        series[64 * s : 64 * (s + 1), :] = cols.T[:64]
    sign = jnp.where(lax.broadcasted_iota(jnp.int32, (STN, 8, 128), 1) < PER, 1.0, -1.0)
    for j in range(8):
        near = series[pl.ds(j, 8 * STN, stride=8), :].reshape(STN, 8, 128)
        far = (pltpu.roll(near, PER, 1) * sign).reshape(8 * STN, 128)
        left = jnp.concatenate([near.reshape(8 * STN, 128), far], 1).astype(BF16)
        right = []
        for r in range(2):
            rows = [series[pl.ds(32 * r + 8 * i + j, STN, stride=64), :] for i in range(PER)]
            right.append(jnp.concatenate(rows, 0))
        right = jnp.concatenate(right, 1).astype(BF16)
        tile = lax.dot_general(left, right, NT, preferred_element_type=F32) / FRAMES
        tile = tile.reshape(STN, 8, 128)
        plain[:, 8 * j : 8 * j + 8, :] = tile
        most = jnp.maximum(most, jnp.max(jnp.abs(tile), 0))
    top = jnp.max(jnp.max(most, 1, keepdims=True), 0, keepdims=True)
    power = jnp.maximum(jnp.floor(jnp.log2(jnp.maximum(top, 1e-37))) - 14.0, -126.0)
    factor, power = jnp.exp2(-power).reshape(1, 1, 1), power.reshape(1, 1, 1)
    station, row, lane = (lax.broadcasted_iota(jnp.int32, (STN, 8, 128), d) for d in range(3))
    out[:, :8, :] = jnp.where((row == 1) & (lane == station), power, plain[:, :8, :] * factor)
    out[:, 8:, :] = plain[:, 8:, :] * factor


def correlate(x, interpret=False):
    vmem = pl.BlockSpec(memory_space=pltpu.VMEM)
    return pl.pallas_call(
        correlate_body,
        out_shape=jax.ShapeDtypeStruct((STN, 64, 128), F32),
        in_specs=[vmem],
        out_specs=vmem,
        scratch_shapes=[pltpu.VMEM((64 * STN, 128), F32), pltpu.VMEM((STN, 64, 128), F32)],
        compiler_params=PARAMS,
        interpret=interpret,
        name="correlate",
    )(x)


def deliver_body(station, x, out, wide, order):
    here = x[:, :8, :]
    line, lane = (lax.broadcasted_iota(jnp.int32, (N1, 8, 128), d) for d in (1, 2))
    holder = (line == 1) & (lane == station[0])
    mirror = (line == 0) & (lane == station[0] + STN)

    def pick(mask):
        return jnp.sum(jnp.sum(jnp.where(mask, here, 0.0), 1, keepdims=True), 2, keepdims=True)

    factor = jnp.exp2(pick(holder))
    wide[...] = x[...] * factor
    wide[:, :8, :] = jnp.where(holder, pick(mirror), here) * factor
    flat = wide.reshape(64 * N1, 128)
    for row in range(8):
        for half in range(2):
            rows = [flat[pl.ds(8 * j + row, N1, stride=64), :] for j in range(4 * half, 4 * half + 4)]
            cols = jnp.concatenate(rows, 0).T
            base = 128 * (2 * row + half)
            for i in range(PER):
                order[pl.ds(base + i, STN, stride=PER), :] = cols[STN * i : STN * (i + 1)]
            out[row // PER, row % PER, :, 128 * half : 128 * (half + 1)] = order[base : base + 128, :]


def deliver(station, x, interpret=False):
    vmem = pl.BlockSpec(memory_space=pltpu.VMEM)
    return pl.pallas_call(
        deliver_body,
        out_shape=jax.ShapeDtypeStruct((2, PER, 128, 256), F32),
        in_specs=[pl.BlockSpec(memory_space=pltpu.SMEM), vmem],
        out_specs=vmem,
        scratch_shapes=[pltpu.VMEM((N1, 64, 128), F32), pltpu.VMEM((16 * 128, 128), F32)],
        compiler_params=PARAMS,
        interpret=interpret,
        name="deliver",
    )(station, x)


def last_frames(frames):
    q = Q // X * lax.axis_index("x") + lax.axis_index("c")
    rounds = []
    for r in range(X):
        piece = lax.dynamic_index_in_dim(frames, (q + r) % X, 1, False)
        pairs = [(s, Q // X * ((s + r) % X)) for s in range(Q - 3, Q)]
        rounds.append(lax.ppermute(piece, ("zh", "x", "c"), pairs))
    rounds = jnp.stack(rounds)
    parts = [
        lax.dynamic_index_in_dim(rounds, (lax.axis_index("x") - s) % X, 0, False) for s in range(Q - 3, Q)
    ]
    last = jnp.concatenate([parts[0][:, 3:], parts[1], parts[2]], 1)
    return lax.ppermute(last, ("zh", "x", "c"), [(Q // X * x, Q + Q // X * x) for x in range(X)])


def shards(voltages):
    frames = voltages.reshape(2, PER, SENT, N1, N2)
    hist = last_frames(frames)
    doubled = jnp.repeat(frames.transpose(1, 0, 2, 3, 4), Q // X, 0)
    half = lax.all_to_all(doubled, ("x", "c"), 0, 0, tiled=True)
    core = lax.axis_index("c").astype(jnp.int32).reshape(1)
    station = lax.axis_index("stn").astype(jnp.int32).reshape(1)
    spectra = channelise((core, station), half, hist)
    spectra = lax.all_to_all(spectra.reshape(Q, 2 * N2 // Q, N1 * BLOCK), ("x", "c"), 0, 0, tiled=True)
    spectra = regroup(spectra).reshape(STN * ZH, BLOCK, 128)
    spectra = lax.all_to_all(spectra, ("stn", "zh"), 0, 0, tiled=True)
    products = correlate(spectra.reshape(STN, ZH, BLOCK, 128))
    products = lax.all_to_all(products.astype(jnp.float16), "stn", 0, 0, tiled=True)
    return deliver(station, products.astype(F32))


def solution(mesh):
    split = Mesh(mesh.devices.reshape(STN, ZH, X, Q // X), ("stn", "zh", "x", "c"))
    in_specs = (P(None, "stn", ("zh", "x", "c")),)
    out_specs = P(None, "stn", None, ("zh", "x", "c"))
    return jax.shard_map(shards, mesh=split, in_specs=in_specs, out_specs=out_specs, check_vma=False)
```

```python
import math

import jax
import jax.numpy as jnp
import ml_dtypes
import numpy as np
from jax import lax
from jax.experimental import pallas as pl
from jax.experimental.pallas import tpu as pltpu
from jax.sharding import Mesh
from jax.sharding import PartitionSpec as P

TAPS = 16
NCH = 4096
N1, N2 = 32, 128
STN, ZH, X, Q = 32, 2, 4, 8
FRAMES = 96
BLOCK = 24
HIST = TAPS - 1
LATE = 8
FEW = BLOCK - LATE
SENT = 6
PER = 4
PARAMS = pltpu.CompilerParams(vmem_limit_bytes=48 * 1024 * 1024)
F32, BF16 = jnp.float32, jnp.bfloat16
NT = (((1,), (1,)), ((), ()))


def prototype():
    index = np.arange(TAPS * NCH, dtype=np.float64)
    window = 0.5 - 0.5 * np.cos(2.0 * math.pi * (index + 0.5) / (TAPS * NCH))
    taps = np.sinc((index + 0.5 - TAPS * NCH / 2) / NCH) * window
    return taps.astype(np.float32).reshape(TAPS, N1, N2)


def halves(table):
    high = table.astype(ml_dtypes.bfloat16)
    low = (table - high.astype(np.float64)).astype(ml_dtypes.bfloat16)
    return high, low


def complex_block(angle):
    c, s = np.cos(angle), np.sin(angle)
    return np.block([[c, s], [-s, c]])


def tables():
    k1, k2 = np.arange(N1), np.arange(N2)
    first = complex_block(2 * math.pi * (np.outer(k1, k1) % N1) / N1)
    second = complex_block(2 * math.pi * (np.outer(k2, k2) % N2) / N2) / 64.0
    second = second.reshape(2, ZH, Q, 8, 2 * N2).transpose(2, 1, 0, 3, 4).reshape(2 * N2, 2 * N2)
    turn = 2 * math.pi * np.outer(k1, k2) / NCH
    first = np.concatenate(halves(first), 0)
    second = np.concatenate(halves(second), 0)
    twiddle = np.stack([np.cos(turn), np.sin(turn)]).astype(np.float32)
    return first, second, twiddle


def spectrum(filtered, count, first, second, twiddle, stage, turned_re, turned_im, out):
    def pair(step, carry):
        for half in range(2):
            for r in range(2):
                stage[N1 * r : N1 * (r + 1), N2 * half : N2 * (half + 1)] = filtered(r, 2 * step + half).astype(BF16)
        both = jnp.dot(first[...], stage[...], preferred_element_type=F32)
        both = both[: 2 * N1] + both[2 * N1 :]
        for half in range(2):
            re = both[:N1, N2 * half : N2 * (half + 1)]
            im = both[N1:, N2 * half : N2 * (half + 1)]
            rows = pl.ds(2 * step + half, N1, stride=count)
            turned_re[rows, :] = re * twiddle[0] + im * twiddle[1]
            turned_im[rows, :] = im * twiddle[0] - re * twiddle[1]
        return carry

    lax.fori_loop(0, count // 2, pair, 0)
    for t in range(N1 * count // 256):
        rows = slice(256 * t, 256 * (t + 1))
        value = jnp.concatenate([turned_re[rows], turned_im[rows]], 1)
        high = value.astype(BF16)
        low = (value - high.astype(F32)).astype(BF16)
        both = lax.dot_general(second[...], high, NT, preferred_element_type=F32)
        rest = lax.dot_general(second[: 2 * N2], low, NT, preferred_element_type=F32)
        out[:, rows] = (both[: 2 * N2] + (both[2 * N2 :] + rest)).astype(BF16)


def early_body(core, column, station, *refs):
    pieces, refs = refs[:Q], refs[Q:]
    taps, first, second, twiddle, sums, out, frames, stage, turned_re, turned_im = refs
    start = BLOCK * core[0]
    for r in range(2):
        frames[r, :HIST] = jnp.zeros((HIST, N1, N2), F32)
        for p in range(Q):
            shard = Q // X * ((column[0] + X - p // 2) % X) + (core[0] + p) % 2
            frames[r, pl.ds(HIST + SENT * shard, SENT)] = pieces[p][r].astype(F32)

    def filtered(r, f):
        acc = taps[0] * frames[r, start + f]
        for k in range(1, TAPS):
            acc = acc + taps[k] * frames[r, start + f + k]
        return acc

    def keep(f, carry):
        for r in range(2):
            sums[r, f] = filtered(r, f)
        return carry

    lax.fori_loop(0, FEW, keep, 0)
    late = lambda r, f: filtered(r, FEW + f)
    spectrum(late, LATE, first, second, twiddle, stage, turned_re, turned_im, out)


def rest_body(core, column, station, sums, hist, done, taps, first, second, twiddle, out, total, past, stage, turned_re, turned_im):
    out[:, N1 * FEW :] = done[...]
    total[...] = sums[...]

    @pl.when(core[0] == 0)
    def _():
        past[...] = hist[...].astype(F32)
        for f in range(HIST):
            for r in range(2):
                acc = sums[r, f]
                for k in range(HIST - f):
                    acc = acc + taps[k] * past[r, f + k]
                total[r, f] = acc

    spectrum(lambda r, f: total[r, f], FEW, first, second, twiddle, stage, turned_re, turned_im, out)


def kernel(body, scalars, args, out_shape, scratch, frames, name, interpret):
    vmem = pl.BlockSpec(memory_space=pltpu.VMEM)
    scratch = scratch + [
        pltpu.VMEM((2 * N1, 2 * N2), BF16),
        pltpu.VMEM((N1 * frames, N2), F32),
        pltpu.VMEM((N1 * frames, N2), F32),
    ]
    return pl.pallas_call(
        body,
        out_shape=out_shape,
        in_specs=[pl.BlockSpec(memory_space=pltpu.SMEM)] * len(scalars) + [vmem] * len(args),
        out_specs=jax.tree.map(lambda _: vmem, out_shape),
        scratch_shapes=scratch,
        compiler_params=PARAMS,
        interpret=interpret,
        name=name,
    )(*scalars, *args)


def channelise(scalars, pieces, hist, interpret=False):
    fixed = [jnp.asarray(a) for a in (prototype(), *tables())]
    shape = jax.ShapeDtypeStruct
    outs = (shape((2, FEW, N1, N2), F32), shape((2 * N2, N1 * LATE), BF16))
    scratch = [pltpu.VMEM((2, HIST + Q * SENT, N1, N2), F32)]
    sums, done = kernel(early_body, scalars, (*pieces, *fixed), outs, scratch, LATE, "early", interpret)
    outs = shape((2 * N2, N1 * BLOCK), BF16)
    scratch = [pltpu.VMEM((2, FEW, N1, N2), F32), pltpu.VMEM((2, HIST, N1, N2), F32)]
    return kernel(rest_body, scalars, (sums, hist, done, *fixed), outs, scratch, FEW, "rest", interpret)


def regroup_body(x, out):
    for z in range(ZH):
        pieces = []
        for c in range(2):
            for r in range(2):
                for i in range(PER):
                    pair = x[2 * i + c, 16 * z : 16 * z + 16, :].astype(F32)
                    pieces.append(pair[8 * r : 8 * r + 8])
        for t in range(N1 * BLOCK // 128):
            piece = jnp.concatenate([p[:, 128 * t : 128 * (t + 1)] for p in pieces], 0).T
            for part in range(16):
                k, f = divmod(128 * t + 8 * part, FEW)
                if k >= N1:
                    k, f = 16 * t + part - N1 * FEW // 8, FEW
                out[k, z, f : f + 8, :] = piece[8 * part : 8 * part + 8].astype(BF16)


def regroup(x, interpret=False):
    vmem = pl.BlockSpec(memory_space=pltpu.VMEM)
    return pl.pallas_call(
        regroup_body,
        out_shape=jax.ShapeDtypeStruct((STN, ZH, BLOCK, 128), BF16),
        in_specs=[vmem],
        out_specs=vmem,
        compiler_params=PARAMS,
        interpret=interpret,
        name="regroup",
    )(x)


def correlate_body(x, out, series, plain):
    most = jnp.zeros((8, 128), F32)
    zero = jnp.zeros((128 - FRAMES, 128), F32)
    for s in range(STN):
        both = jnp.concatenate([x[s, 0].astype(F32), x[s, 1].astype(F32)], 0)
        cols = jnp.concatenate([both, pltpu.roll(both, 64, 1), zero], 0)
        series[64 * s : 64 * (s + 1), :] = cols.T[:64]
    sign = jnp.where(lax.broadcasted_iota(jnp.int32, (STN, 8, 128), 1) < PER, 1.0, -1.0)
    for j in range(8):
        near = series[pl.ds(j, 8 * STN, stride=8), :].reshape(STN, 8, 128)
        far = (pltpu.roll(near, PER, 1) * sign).reshape(8 * STN, 128)
        left = jnp.concatenate([near.reshape(8 * STN, 128), far], 1).astype(BF16)
        right = []
        for r in range(2):
            rows = [series[pl.ds(32 * r + 8 * i + j, STN, stride=64), :] for i in range(PER)]
            right.append(jnp.concatenate(rows, 0))
        right = jnp.concatenate(right, 1).astype(BF16)
        tile = lax.dot_general(left, right, NT, preferred_element_type=F32) / FRAMES
        tile = tile.reshape(STN, 8, 128)
        plain[:, 8 * j : 8 * j + 8, :] = tile
        most = jnp.maximum(most, jnp.max(jnp.abs(tile), 0))
    top = jnp.max(jnp.max(most, 1, keepdims=True), 0, keepdims=True)
    power = jnp.maximum(jnp.floor(jnp.log2(jnp.maximum(top, 1e-37))) - 14.0, -126.0)
    factor, power = jnp.exp2(-power).reshape(1, 1, 1), power.reshape(1, 1, 1)
    station, row, lane = (lax.broadcasted_iota(jnp.int32, (STN, 8, 128), d) for d in range(3))
    out[:, :8, :] = jnp.where((row == 1) & (lane == station), power, plain[:, :8, :] * factor)
    out[:, 8:, :] = plain[:, 8:, :] * factor


def correlate(x, interpret=False):
    vmem = pl.BlockSpec(memory_space=pltpu.VMEM)
    return pl.pallas_call(
        correlate_body,
        out_shape=jax.ShapeDtypeStruct((STN, 64, 128), F32),
        in_specs=[vmem],
        out_specs=vmem,
        scratch_shapes=[pltpu.VMEM((64 * STN, 128), F32), pltpu.VMEM((STN, 64, 128), F32)],
        compiler_params=PARAMS,
        interpret=interpret,
        name="correlate",
    )(x)


def deliver_body(station, x, out, wide, order):
    here = x[:, :8, :]
    line, lane = (lax.broadcasted_iota(jnp.int32, (N1, 8, 128), d) for d in (1, 2))
    holder = (line == 1) & (lane == station[0])
    mirror = (line == 0) & (lane == station[0] + STN)

    def pick(mask):
        return jnp.sum(jnp.sum(jnp.where(mask, here, 0.0), 1, keepdims=True), 2, keepdims=True)

    factor = jnp.exp2(pick(holder))
    wide[...] = x[...] * factor
    wide[:, :8, :] = jnp.where(holder, pick(mirror), here) * factor
    flat = wide.reshape(64 * N1, 128)
    for row in range(8):
        for half in range(2):
            rows = [flat[pl.ds(8 * j + row, N1, stride=64), :] for j in range(4 * half, 4 * half + 4)]
            cols = jnp.concatenate(rows, 0).T
            base = 128 * (2 * row + half)
            for i in range(PER):
                order[pl.ds(base + i, STN, stride=PER), :] = cols[STN * i : STN * (i + 1)]
            out[row // PER, row % PER, :, 128 * half : 128 * (half + 1)] = order[base : base + 128, :]


def deliver(station, x, interpret=False):
    vmem = pl.BlockSpec(memory_space=pltpu.VMEM)
    return pl.pallas_call(
        deliver_body,
        out_shape=jax.ShapeDtypeStruct((2, PER, 128, 256), F32),
        in_specs=[pl.BlockSpec(memory_space=pltpu.SMEM), vmem],
        out_specs=vmem,
        scratch_shapes=[pltpu.VMEM((N1, 64, 128), F32), pltpu.VMEM((16 * 128, 128), F32)],
        compiler_params=PARAMS,
        interpret=interpret,
        name="deliver",
    )(station, x)


def last_frames(frames):
    q = Q // X * lax.axis_index("x") + lax.axis_index("c")
    rounds = []
    for r in range(X):
        piece = lax.dynamic_index_in_dim(frames, (q + r) % X, 1, False)
        pairs = [(s, Q // X * ((s + r) % X)) for s in range(Q - 3, Q)]
        rounds.append(lax.ppermute(piece, ("zh", "x", "c"), pairs))
    rounds = jnp.stack(rounds)
    parts = [
        lax.dynamic_index_in_dim(rounds, (lax.axis_index("x") - s) % X, 0, False) for s in range(Q - 3, Q)
    ]
    last = jnp.concatenate([parts[0][:, 3:], parts[1], parts[2]], 1)
    return lax.ppermute(last, ("zh", "x", "c"), [(Q // X * x, Q + Q // X * x) for x in range(X)])


def half_of_input(frames):
    pieces = []
    for p in range(Q):
        dx, dc = divmod(p, 2)
        piece = lax.dynamic_index_in_dim(frames, (lax.axis_index("x") + dx) % X, 1, False)
        pairs = [(2 * x + c, 2 * ((x + dx) % X) + (c + dc) % 2) for x in range(X) for c in range(2)]
        pieces.append(lax.ppermute(piece, ("x", "c"), pairs) if p else piece)
    return pieces


def shards(voltages):
    frames = voltages.reshape(2, PER, SENT, N1, N2)
    hist = last_frames(frames)
    pieces = half_of_input(frames)
    scalars = [lax.axis_index(name).astype(jnp.int32).reshape(1) for name in ("c", "x", "stn")]
    spectra = channelise(scalars, pieces, hist)
    spectra = lax.all_to_all(spectra.reshape(Q, 2 * N2 // Q, N1 * BLOCK), ("x", "c"), 0, 0, tiled=True)
    spectra = regroup(spectra).reshape(STN * ZH, BLOCK, 128)
    spectra = lax.all_to_all(spectra, ("stn", "zh"), 0, 0, tiled=True)
    products = correlate(spectra.reshape(STN, ZH, BLOCK, 128))
    products = lax.all_to_all(products.astype(jnp.float16), "stn", 0, 0, tiled=True)
    return deliver(scalars[2], products.astype(F32))


def solution(mesh):
    split = Mesh(mesh.devices.reshape(STN, ZH, X, Q // X), ("stn", "zh", "x", "c"))
    in_specs = (P(None, "stn", ("zh", "x", "c")),)
    out_specs = P(None, "stn", None, ("zh", "x", "c"))
    return jax.shard_map(shards, mesh=split, in_specs=in_specs, out_specs=out_specs, check_vma=False)
```

```python
import math

import jax
import jax.numpy as jnp
import ml_dtypes
import numpy as np
from jax import lax
from jax.experimental import pallas as pl
from jax.experimental.pallas import tpu as pltpu
from jax.sharding import Mesh
from jax.sharding import PartitionSpec as P

TAPS = 16
NCH = 4096
N1, N2 = 32, 128
STN, ZH, X, Q = 32, 2, 4, 8
FRAMES = 96
BLOCK = 24
HIST = TAPS - 1
LATE = 8
FEW = BLOCK - LATE
SENT = 6
PER = 4
PARAMS = pltpu.CompilerParams(vmem_limit_bytes=48 * 1024 * 1024)
F32, BF16 = jnp.float32, jnp.bfloat16
NT = (((1,), (1,)), ((), ()))


def prototype():
    index = np.arange(TAPS * NCH, dtype=np.float64)
    window = 0.5 - 0.5 * np.cos(2.0 * math.pi * (index + 0.5) / (TAPS * NCH))
    taps = np.sinc((index + 0.5 - TAPS * NCH / 2) / NCH) * window
    return taps.astype(np.float32).reshape(TAPS, N1, N2)


def halves(table):
    high = table.astype(ml_dtypes.bfloat16)
    low = (table - high.astype(np.float64)).astype(ml_dtypes.bfloat16)
    return high, low


def complex_block(angle):
    c, s = np.cos(angle), np.sin(angle)
    return np.block([[c, s], [-s, c]])


def tables():
    k1, k2 = np.arange(N1), np.arange(N2)
    first = complex_block(2 * math.pi * (np.outer(k1, k1) % N1) / N1)
    second = complex_block(2 * math.pi * (np.outer(k2, k2) % N2) / N2) / 64.0
    second = second.reshape(2, ZH, Q, 8, 2 * N2).transpose(2, 1, 0, 3, 4).reshape(2 * N2, 2 * N2)
    turn = 2 * math.pi * np.outer(k1, k2) / NCH
    first = np.concatenate(halves(first), 0)
    second = np.concatenate(halves(second), 0)
    twiddle = np.stack([np.cos(turn), np.sin(turn)]).astype(np.float32)
    return first, second, twiddle


def spectrum(filtered, count, first, second, twiddle, stage, turned_re, turned_im, out):
    def pair(step, carry):
        for half in range(2):
            for r in range(2):
                stage[N1 * r : N1 * (r + 1), N2 * half : N2 * (half + 1)] = filtered(r, 2 * step + half).astype(BF16)
        both = jnp.dot(first[...], stage[...], preferred_element_type=F32)
        both = both[: 2 * N1] + both[2 * N1 :]
        for half in range(2):
            re = both[:N1, N2 * half : N2 * (half + 1)]
            im = both[N1:, N2 * half : N2 * (half + 1)]
            rows = pl.ds(2 * step + half, N1, stride=count)
            turned_re[rows, :] = re * twiddle[0] + im * twiddle[1]
            turned_im[rows, :] = im * twiddle[0] - re * twiddle[1]
        return carry

    lax.fori_loop(0, count // 2, pair, 0)
    for t in range(N1 * count // 256):
        rows = slice(256 * t, 256 * (t + 1))
        value = jnp.concatenate([turned_re[rows], turned_im[rows]], 1)
        high = value.astype(BF16)
        low = (value - high.astype(F32)).astype(BF16)
        both = lax.dot_general(second[...], high, NT, preferred_element_type=F32)
        rest = lax.dot_general(second[: 2 * N2], low, NT, preferred_element_type=F32)
        out[:, rows] = (both[: 2 * N2] + (both[2 * N2 :] + rest)).astype(BF16)


def early_body(place, station, *refs):
    pieces, refs = refs[:PER], refs[PER:]
    taps, first, second, twiddle, sums, out, frames, stage, turned_re, turned_im = refs
    for r in range(2):
        frames[r, :HIST] = jnp.zeros((HIST, N1, N2), F32)
        for p in range(PER):
            shard = jnp.bitwise_xor(place[0] % PER, p)
            frames[r, pl.ds(HIST + SENT * shard, SENT)] = pieces[p][r].astype(F32)

    def filtered(r, f):
        acc = taps[0] * frames[r, f]
        for k in range(1, TAPS):
            acc = acc + taps[k] * frames[r, f + k]
        return acc

    def keep(f, carry):
        for r in range(2):
            sums[r, f] = filtered(r, f)
        return carry

    lax.fori_loop(0, FEW, keep, 0)
    late = lambda r, f: filtered(r, FEW + f)
    spectrum(late, LATE, first, second, twiddle, stage, turned_re, turned_im, out)


def rest_body(place, station, sums, far, near, done, taps, first, second, twiddle, out, total, past, stage, turned_re, turned_im):
    out[:, N1 * FEW :] = done[...]

    @pl.when(place[0] < PER)
    def _():
        past[...] = far[...].astype(F32)

    @pl.when(place[0] >= PER)
    def _():
        past[...] = near[...].astype(F32)

    for r in range(2):
        for f in range(HIST):
            acc = sums[r, f]
            for k in range(HIST - f):
                acc = acc + taps[k] * past[r, f + k]
            total[r, f] = acc
        total[r, HIST:] = sums[r, HIST:]

    spectrum(lambda r, f: total[r, f], FEW, first, second, twiddle, stage, turned_re, turned_im, out)


def kernel(body, scalars, args, out_shape, scratch, frames, name, interpret):
    vmem = pl.BlockSpec(memory_space=pltpu.VMEM)
    scratch = scratch + [
        pltpu.VMEM((2 * N1, 2 * N2), BF16),
        pltpu.VMEM((N1 * frames, N2), F32),
        pltpu.VMEM((N1 * frames, N2), F32),
    ]
    return pl.pallas_call(
        body,
        out_shape=out_shape,
        in_specs=[pl.BlockSpec(memory_space=pltpu.SMEM)] * len(scalars) + [vmem] * len(args),
        out_specs=jax.tree.map(lambda _: vmem, out_shape),
        scratch_shapes=scratch,
        compiler_params=PARAMS,
        interpret=interpret,
        name=name,
    )(*scalars, *args)


def channelise(scalars, pieces, far, near, interpret=False):
    fixed = [jnp.asarray(a) for a in (prototype(), *tables())]
    shape = jax.ShapeDtypeStruct
    outs = (shape((2, FEW, N1, N2), F32), shape((2 * N2, N1 * LATE), BF16))
    scratch = [pltpu.VMEM((2, HIST + BLOCK, N1, N2), F32)]
    sums, done = kernel(early_body, scalars, (*pieces, *fixed), outs, scratch, LATE, "early", interpret)
    outs = shape((2 * N2, N1 * BLOCK), BF16)
    scratch = [pltpu.VMEM((2, FEW, N1, N2), F32), pltpu.VMEM((2, HIST, N1, N2), F32)]
    return kernel(rest_body, scalars, (sums, far, near, done, *fixed), outs, scratch, FEW, "rest", interpret)


def regroup_body(x, out):
    for z in range(ZH):
        pieces = []
        for c in range(2):
            for r in range(2):
                for i in range(PER):
                    pair = x[PER * c + i, 16 * z : 16 * z + 16, :].astype(F32)
                    pieces.append(pair[8 * r : 8 * r + 8])
        for t in range(N1 * BLOCK // 128):
            piece = jnp.concatenate([p[:, 128 * t : 128 * (t + 1)] for p in pieces], 0).T
            for part in range(16):
                k, f = divmod(128 * t + 8 * part, FEW)
                if k >= N1:
                    k, f = 16 * t + part - N1 * FEW // 8, FEW
                out[k, z, f : f + 8, :] = piece[8 * part : 8 * part + 8].astype(BF16)


def regroup(x, interpret=False):
    vmem = pl.BlockSpec(memory_space=pltpu.VMEM)
    return pl.pallas_call(
        regroup_body,
        out_shape=jax.ShapeDtypeStruct((STN, ZH, BLOCK, 128), BF16),
        in_specs=[vmem],
        out_specs=vmem,
        compiler_params=PARAMS,
        interpret=interpret,
        name="regroup",
    )(x)


def correlate_body(x, out, series, plain):
    most = jnp.zeros((8, 128), F32)
    zero = jnp.zeros((128 - FRAMES, 128), F32)
    for s in range(STN):
        both = jnp.concatenate([x[s, 0].astype(F32), x[s, 1].astype(F32)], 0)
        cols = jnp.concatenate([both, pltpu.roll(both, 64, 1), zero], 0)
        series[64 * s : 64 * (s + 1), :] = cols.T[:64]
    sign = jnp.where(lax.broadcasted_iota(jnp.int32, (STN, 8, 128), 1) < PER, 1.0, -1.0)
    for j in range(8):
        near = series[pl.ds(j, 8 * STN, stride=8), :].reshape(STN, 8, 128)
        far = (pltpu.roll(near, PER, 1) * sign).reshape(8 * STN, 128)
        left = jnp.concatenate([near.reshape(8 * STN, 128), far], 1).astype(BF16)
        right = []
        for r in range(2):
            rows = [series[pl.ds(32 * r + 8 * i + j, STN, stride=64), :] for i in range(PER)]
            right.append(jnp.concatenate(rows, 0))
        right = jnp.concatenate(right, 1).astype(BF16)
        tile = lax.dot_general(left, right, NT, preferred_element_type=F32) / FRAMES
        tile = tile.reshape(STN, 8, 128)
        plain[:, 8 * j : 8 * j + 8, :] = tile
        most = jnp.maximum(most, jnp.max(jnp.abs(tile), 0))
    top = jnp.max(jnp.max(most, 1, keepdims=True), 0, keepdims=True)
    power = jnp.maximum(jnp.floor(jnp.log2(jnp.maximum(top, 1e-37))) - 14.0, -126.0)
    factor, power = jnp.exp2(-power).reshape(1, 1, 1), power.reshape(1, 1, 1)
    station, row, lane = (lax.broadcasted_iota(jnp.int32, (STN, 8, 128), d) for d in range(3))
    out[:, :8, :] = jnp.where((row == 1) & (lane == station), power, plain[:, :8, :] * factor)
    out[:, 8:, :] = plain[:, 8:, :] * factor


def correlate(x, interpret=False):
    vmem = pl.BlockSpec(memory_space=pltpu.VMEM)
    return pl.pallas_call(
        correlate_body,
        out_shape=jax.ShapeDtypeStruct((STN, 64, 128), F32),
        in_specs=[vmem],
        out_specs=vmem,
        scratch_shapes=[pltpu.VMEM((64 * STN, 128), F32), pltpu.VMEM((STN, 64, 128), F32)],
        compiler_params=PARAMS,
        interpret=interpret,
        name="correlate",
    )(x)


def deliver_body(station, x, out, wide, order):
    here = x[:, :8, :]
    line, lane = (lax.broadcasted_iota(jnp.int32, (N1, 8, 128), d) for d in (1, 2))
    holder = (line == 1) & (lane == station[0])
    mirror = (line == 0) & (lane == station[0] + STN)

    def pick(mask):
        return jnp.sum(jnp.sum(jnp.where(mask, here, 0.0), 1, keepdims=True), 2, keepdims=True)

    factor = jnp.exp2(pick(holder))
    wide[...] = x[...] * factor
    wide[:, :8, :] = jnp.where(holder, pick(mirror), here) * factor
    flat = wide.reshape(64 * N1, 128)
    for row in range(8):
        for half in range(2):
            rows = [flat[pl.ds(8 * j + row, N1, stride=64), :] for j in range(4 * half, 4 * half + 4)]
            cols = jnp.concatenate(rows, 0).T
            base = 128 * (2 * row + half)
            for i in range(PER):
                order[pl.ds(base + i, STN, stride=PER), :] = cols[STN * i : STN * (i + 1)]
            out[row // PER, row % PER, :, 128 * half : 128 * (half + 1)] = order[base : base + 128, :]


def deliver(station, x, interpret=False):
    vmem = pl.BlockSpec(memory_space=pltpu.VMEM)
    return pl.pallas_call(
        deliver_body,
        out_shape=jax.ShapeDtypeStruct((2, PER, 128, 256), F32),
        in_specs=[pl.BlockSpec(memory_space=pltpu.SMEM), vmem],
        out_specs=vmem,
        scratch_shapes=[pltpu.VMEM((N1, 64, 128), F32), pltpu.VMEM((16 * 128, 128), F32)],
        compiler_params=PARAMS,
        interpret=interpret,
        name="deliver",
    )(station, x)


def last_frames(frames, place):
    rounds = []
    for r in range(X):
        piece = lax.dynamic_index_in_dim(frames, (place + r) % X, 1, False)
        pairs = [(s, Q // X * ((s + r) % X)) for s in range(Q - 3, Q)]
        rounds.append(lax.ppermute(piece, ("zh", "x", "c"), pairs))
    rounds = jnp.stack(rounds)
    parts = [
        lax.dynamic_index_in_dim(rounds, (lax.axis_index("x") - s) % X, 0, False) for s in range(Q - 3, Q)
    ]
    last = jnp.concatenate([parts[0][:, 3:], parts[1], parts[2]], 1)
    last, frames = lax.optimization_barrier((last, frames))
    return lax.ppermute(last, ("zh", "x", "c"), [(Q // X * i, Q + i) for i in range(PER)]), frames


def block_of_input(frames, place):
    pieces = []
    for p in range(PER):
        piece = lax.dynamic_index_in_dim(frames, (place % PER) ^ p, 1, False)
        pairs = [(t, t ^ p) for t in range(Q)]
        pieces.append(lax.ppermute(piece, ("x", "c"), pairs) if p else piece)
    return pieces


def shards(voltages):
    frames = voltages.reshape(2, PER, SENT, N1, N2)
    place = Q // X * lax.axis_index("x") + lax.axis_index("c")
    far, frames = last_frames(frames, place)
    pieces = block_of_input(frames, place)
    parts = [lax.dynamic_index_in_dim(jnp.stack(pieces), (place % PER) ^ s, 0, False) for s in (1, 2, 3)]
    last = jnp.concatenate([parts[0][:, 3:], parts[1], parts[2]], 1)
    near = lax.ppermute(last, ("x", "c"), [(t, t + PER) for t in range(PER)])
    scalars = [a.astype(jnp.int32).reshape(1) for a in (place, lax.axis_index("stn"))]
    spectra = channelise(scalars, pieces, far, near)
    spectra = lax.all_to_all(spectra.reshape(Q, 2 * N2 // Q, N1 * BLOCK), ("x", "c"), 0, 0, tiled=True)
    spectra = regroup(spectra).reshape(STN * ZH, BLOCK, 128)
    spectra = lax.all_to_all(spectra, ("stn", "zh"), 0, 0, tiled=True)
    products = correlate(spectra.reshape(STN, ZH, BLOCK, 128))
    products = lax.all_to_all(products.astype(jnp.float16), "stn", 0, 0, tiled=True)
    return deliver(scalars[1], products.astype(F32))


def solution(mesh):
    split = Mesh(mesh.devices.reshape(STN, ZH, X, Q // X), ("stn", "zh", "x", "c"))
    in_specs = (P(None, "stn", ("zh", "x", "c")),)
    out_specs = P(None, "stn", None, ("zh", "x", "c"))
    return jax.shard_map(shards, mesh=split, in_specs=in_specs, out_specs=out_specs, check_vma=False)
```

```python
import math

import jax
import jax.numpy as jnp
import ml_dtypes
import numpy as np
from jax import lax
from jax.experimental import pallas as pl
from jax.experimental.pallas import tpu as pltpu
from jax.sharding import Mesh
from jax.sharding import PartitionSpec as P

TAPS = 16
NCH = 4096
N1, N2 = 32, 128
STN, ZH, X, Q = 32, 2, 4, 8
FRAMES = 96
BLOCK = 24
HIST = TAPS - 1
LATE = 8
FEW = BLOCK - LATE
SENT = 6
PER = 4
PARAMS = pltpu.CompilerParams(vmem_limit_bytes=48 * 1024 * 1024)
F32, BF16 = jnp.float32, jnp.bfloat16
NT = (((1,), (1,)), ((), ()))


def prototype():
    index = np.arange(TAPS * NCH, dtype=np.float64)
    window = 0.5 - 0.5 * np.cos(2.0 * math.pi * (index + 0.5) / (TAPS * NCH))
    taps = np.sinc((index + 0.5 - TAPS * NCH / 2) / NCH) * window
    return taps.astype(np.float32).reshape(TAPS, N1, N2)


def halves(table):
    high = table.astype(ml_dtypes.bfloat16)
    low = (table - high.astype(np.float64)).astype(ml_dtypes.bfloat16)
    return high, low


def complex_block(angle):
    c, s = np.cos(angle), np.sin(angle)
    return np.block([[c, s], [-s, c]])


def tables():
    k1, k2 = np.arange(N1), np.arange(N2)
    first = complex_block(2 * math.pi * (np.outer(k1, k1) % N1) / N1)
    second = complex_block(2 * math.pi * (np.outer(k2, k2) % N2) / N2) / 64.0
    second = second.reshape(2, ZH, Q, 8, 2 * N2).transpose(2, 1, 0, 3, 4).reshape(2 * N2, 2 * N2)
    turn = 2 * math.pi * np.outer(k1, k2) / NCH
    first = np.concatenate(halves(first), 0)
    second = np.concatenate(halves(second), 0)
    twiddle = np.stack([np.cos(turn), np.sin(turn)]).astype(np.float32)
    return first, second, twiddle


def spectrum(filtered, count, first, second, twiddle, stage, turned_re, turned_im, out):
    def pair(step, carry):
        for half in range(2):
            for r in range(2):
                stage[N1 * r : N1 * (r + 1), N2 * half : N2 * (half + 1)] = filtered(r, 2 * step + half).astype(BF16)
        both = jnp.dot(first[...], stage[...], preferred_element_type=F32)
        both = both[: 2 * N1] + both[2 * N1 :]
        for half in range(2):
            re = both[:N1, N2 * half : N2 * (half + 1)]
            im = both[N1:, N2 * half : N2 * (half + 1)]
            rows = pl.ds(2 * step + half, N1, stride=count)
            turned_re[rows, :] = re * twiddle[0] + im * twiddle[1]
            turned_im[rows, :] = im * twiddle[0] - re * twiddle[1]
        return carry

    lax.fori_loop(0, count // 2, pair, 0)
    for t in range(N1 * count // 256):
        rows = slice(256 * t, 256 * (t + 1))
        value = jnp.concatenate([turned_re[rows], turned_im[rows]], 1)
        high = value.astype(BF16)
        low = (value - high.astype(F32)).astype(BF16)
        both = lax.dot_general(second[...], high, NT, preferred_element_type=F32)
        rest = lax.dot_general(second[: 2 * N2], low, NT, preferred_element_type=F32)
        out[:, rows] = (both[: 2 * N2] + (both[2 * N2 :] + rest)).astype(BF16)


def early_body(core, column, station, *refs):
    pieces, refs = refs[:X], refs[X:]
    taps, first, second, twiddle, sums, out, frames, stage, turned_re, turned_im = refs
    start = BLOCK * core[0]
    for r in range(2):
        frames[r, :HIST] = jnp.zeros((HIST, N1, N2), F32)
        for p in range(Q):
            shard = Q // X * ((column[0] + X - p // 2) % X) + (core[0] + p) % 2
            frames[r, pl.ds(HIST + SENT * shard, SENT)] = pieces[p // 2][p % 2, r].astype(F32)

    def filtered(r, f):
        acc = taps[0] * frames[r, start + f]
        for k in range(1, TAPS):
            acc = acc + taps[k] * frames[r, start + f + k]
        return acc

    def keep(f, carry):
        for r in range(2):
            sums[r, f] = filtered(r, f)
        return carry

    lax.fori_loop(0, FEW, keep, 0)
    late = lambda r, f: filtered(r, FEW + f)
    spectrum(late, LATE, first, second, twiddle, stage, turned_re, turned_im, out)


def rest_body(core, column, station, sums, hist, done, taps, first, second, twiddle, out, total, past, stage, turned_re, turned_im):
    out[:, N1 * FEW :] = done[...]
    total[...] = sums[...]

    @pl.when(core[0] == 0)
    def _():
        past[...] = hist[...].astype(F32)
        for f in range(HIST):
            for r in range(2):
                acc = sums[r, f]
                for k in range(HIST - f):
                    acc = acc + taps[k] * past[r, f + k]
                total[r, f] = acc

    spectrum(lambda r, f: total[r, f], FEW, first, second, twiddle, stage, turned_re, turned_im, out)


def kernel(body, scalars, args, out_shape, scratch, frames, name, interpret):
    vmem = pl.BlockSpec(memory_space=pltpu.VMEM)
    scratch = scratch + [
        pltpu.VMEM((2 * N1, 2 * N2), BF16),
        pltpu.VMEM((N1 * frames, N2), F32),
        pltpu.VMEM((N1 * frames, N2), F32),
    ]
    return pl.pallas_call(
        body,
        out_shape=out_shape,
        in_specs=[pl.BlockSpec(memory_space=pltpu.SMEM)] * len(scalars) + [vmem] * len(args),
        out_specs=jax.tree.map(lambda _: vmem, out_shape),
        scratch_shapes=scratch,
        compiler_params=PARAMS,
        interpret=interpret,
        name=name,
    )(*scalars, *args)


def channelise(scalars, pieces, hist, interpret=False):
    fixed = [jnp.asarray(a) for a in (prototype(), *tables())]
    shape = jax.ShapeDtypeStruct
    outs = (shape((2, FEW, N1, N2), F32), shape((2 * N2, N1 * LATE), BF16))
    scratch = [pltpu.VMEM((2, HIST + Q * SENT, N1, N2), F32)]
    sums, done = kernel(early_body, scalars, (*pieces, *fixed), outs, scratch, LATE, "early", interpret)
    outs = shape((2 * N2, N1 * BLOCK), BF16)
    scratch = [pltpu.VMEM((2, FEW, N1, N2), F32), pltpu.VMEM((2, HIST, N1, N2), F32)]
    return kernel(rest_body, scalars, (sums, hist, done, *fixed), outs, scratch, FEW, "rest", interpret)


def regroup_body(x, out):
    for z in range(ZH):
        pieces = []
        for c in range(2):
            for r in range(2):
                for i in range(PER):
                    pair = x[2 * i + c, 16 * z : 16 * z + 16, :].astype(F32)
                    pieces.append(pair[8 * r : 8 * r + 8])
        for t in range(N1 * BLOCK // 128):
            piece = jnp.concatenate([p[:, 128 * t : 128 * (t + 1)] for p in pieces], 0).T
            for part in range(16):
                k, f = divmod(128 * t + 8 * part, FEW)
                if k >= N1:
                    k, f = 16 * t + part - N1 * FEW // 8, FEW
                out[k, z, f : f + 8, :] = piece[8 * part : 8 * part + 8].astype(BF16)


def regroup(x, interpret=False):
    vmem = pl.BlockSpec(memory_space=pltpu.VMEM)
    return pl.pallas_call(
        regroup_body,
        out_shape=jax.ShapeDtypeStruct((STN, ZH, BLOCK, 128), BF16),
        in_specs=[vmem],
        out_specs=vmem,
        compiler_params=PARAMS,
        interpret=interpret,
        name="regroup",
    )(x)


def correlate_body(x, out, series, plain):
    most = jnp.zeros((8, 128), F32)
    zero = jnp.zeros((128 - FRAMES, 128), F32)
    for s in range(STN):
        both = jnp.concatenate([x[s, 0].astype(F32), x[s, 1].astype(F32)], 0)
        cols = jnp.concatenate([both, pltpu.roll(both, 64, 1), zero], 0)
        series[64 * s : 64 * (s + 1), :] = cols.T[:64]
    sign = jnp.where(lax.broadcasted_iota(jnp.int32, (STN, 8, 128), 1) < PER, 1.0, -1.0)
    for j in range(8):
        near = series[pl.ds(j, 8 * STN, stride=8), :].reshape(STN, 8, 128)
        far = (pltpu.roll(near, PER, 1) * sign).reshape(8 * STN, 128)
        left = jnp.concatenate([near.reshape(8 * STN, 128), far], 1).astype(BF16)
        right = []
        for r in range(2):
            rows = [series[pl.ds(32 * r + 8 * i + j, STN, stride=64), :] for i in range(PER)]
            right.append(jnp.concatenate(rows, 0))
        right = jnp.concatenate(right, 1).astype(BF16)
        tile = lax.dot_general(left, right, NT, preferred_element_type=F32) / FRAMES
        tile = tile.reshape(STN, 8, 128)
        plain[:, 8 * j : 8 * j + 8, :] = tile
        most = jnp.maximum(most, jnp.max(jnp.abs(tile), 0))
    top = jnp.max(jnp.max(most, 1, keepdims=True), 0, keepdims=True)
    power = jnp.maximum(jnp.floor(jnp.log2(jnp.maximum(top, 1e-37))) - 14.0, -126.0)
    factor, power = jnp.exp2(-power).reshape(1, 1, 1), power.reshape(1, 1, 1)
    station, row, lane = (lax.broadcasted_iota(jnp.int32, (STN, 8, 128), d) for d in range(3))
    out[:, :8, :] = jnp.where((row == 1) & (lane == station), power, plain[:, :8, :] * factor)
    out[:, 8:, :] = plain[:, 8:, :] * factor


def correlate(x, interpret=False):
    vmem = pl.BlockSpec(memory_space=pltpu.VMEM)
    return pl.pallas_call(
        correlate_body,
        out_shape=jax.ShapeDtypeStruct((STN, 64, 128), F32),
        in_specs=[vmem],
        out_specs=vmem,
        scratch_shapes=[pltpu.VMEM((64 * STN, 128), F32), pltpu.VMEM((STN, 64, 128), F32)],
        compiler_params=PARAMS,
        interpret=interpret,
        name="correlate",
    )(x)


def deliver_body(station, x, out, wide, order):
    here = x[:, :8, :]
    line, lane = (lax.broadcasted_iota(jnp.int32, (N1, 8, 128), d) for d in (1, 2))
    holder = (line == 1) & (lane == station[0])
    mirror = (line == 0) & (lane == station[0] + STN)

    def pick(mask):
        return jnp.sum(jnp.sum(jnp.where(mask, here, 0.0), 1, keepdims=True), 2, keepdims=True)

    factor = jnp.exp2(pick(holder))
    wide[...] = x[...] * factor
    wide[:, :8, :] = jnp.where(holder, pick(mirror), here) * factor
    flat = wide.reshape(64 * N1, 128)
    for row in range(8):
        for half in range(2):
            rows = [flat[pl.ds(8 * j + row, N1, stride=64), :] for j in range(4 * half, 4 * half + 4)]
            cols = jnp.concatenate(rows, 0).T
            base = 128 * (2 * row + half)
            for i in range(PER):
                order[pl.ds(base + i, STN, stride=PER), :] = cols[STN * i : STN * (i + 1)]
            out[row // PER, row % PER, :, 128 * half : 128 * (half + 1)] = order[base : base + 128, :]


def deliver(station, x, interpret=False):
    vmem = pl.BlockSpec(memory_space=pltpu.VMEM)
    return pl.pallas_call(
        deliver_body,
        out_shape=jax.ShapeDtypeStruct((2, PER, 128, 256), F32),
        in_specs=[pl.BlockSpec(memory_space=pltpu.SMEM), vmem],
        out_specs=vmem,
        scratch_shapes=[pltpu.VMEM((N1, 64, 128), F32), pltpu.VMEM((16 * 128, 128), F32)],
        compiler_params=PARAMS,
        interpret=interpret,
        name="deliver",
    )(station, x)


def last_frames(frames):
    q = Q // X * lax.axis_index("x") + lax.axis_index("c")
    rounds = []
    for r in range(X):
        piece = lax.dynamic_index_in_dim(frames, (q + r) % X, 1, False)
        pairs = [(s, Q // X * ((s + r) % X)) for s in range(Q - 3, Q)]
        rounds.append(lax.ppermute(piece, ("zh", "x", "c"), pairs))
    rounds = jnp.stack(rounds)
    parts = [
        lax.dynamic_index_in_dim(rounds, (lax.axis_index("x") - s) % X, 0, False) for s in range(Q - 3, Q)
    ]
    last = jnp.concatenate([parts[0][:, 3:], parts[1], parts[2]], 1)
    return lax.ppermute(last, ("zh", "x", "c"), [(Q // X * x, Q + Q // X * x) for x in range(X)])


def half_of_input(frames):
    other = lax.ppermute(frames, "c", [(0, 1), (1, 0)])
    pieces = []
    for p in range(X):
        i = (lax.axis_index("x") + p) % X
        piece = jnp.stack([lax.dynamic_index_in_dim(a, i, 1, False) for a in (frames, other)])
        pieces.append(lax.ppermute(piece, "x", [(x, (x + p) % X) for x in range(X)]) if p else piece)
    return pieces


def shards(voltages):
    frames = voltages.reshape(2, PER, SENT, N1, N2)
    hist = last_frames(frames)
    pieces = half_of_input(frames)
    scalars = [lax.axis_index(name).astype(jnp.int32).reshape(1) for name in ("c", "x", "stn")]
    spectra = channelise(scalars, pieces, hist)
    spectra = lax.all_to_all(spectra.reshape(Q, 2 * N2 // Q, N1 * BLOCK), ("x", "c"), 0, 0, tiled=True)
    spectra = regroup(spectra).reshape(STN * ZH, BLOCK, 128)
    spectra = lax.all_to_all(spectra, ("stn", "zh"), 0, 0, tiled=True)
    products = correlate(spectra.reshape(STN, ZH, BLOCK, 128))
    products = lax.all_to_all(products.astype(jnp.float16), "stn", 0, 0, tiled=True)
    return deliver(scalars[2], products.astype(F32))


def solution(mesh):
    split = Mesh(mesh.devices.reshape(STN, ZH, X, Q // X), ("stn", "zh", "x", "c"))
    in_specs = (P(None, "stn", ("zh", "x", "c")),)
    out_specs = P(None, "stn", None, ("zh", "x", "c"))
    return jax.shard_map(shards, mesh=split, in_specs=in_specs, out_specs=out_specs, check_vma=False)
```

```python
import math

import jax
import jax.numpy as jnp
import ml_dtypes
import numpy as np
from jax import lax
from jax.experimental import pallas as pl
from jax.experimental.pallas import tpu as pltpu
from jax.sharding import Mesh
from jax.sharding import PartitionSpec as P

TAPS = 16
NCH = 4096
N1, N2 = 32, 128
STN, ZH, X, Q = 32, 2, 4, 8
FRAMES = 96
BLOCK = 24
HIST = TAPS - 1
LATE = 8
FEW = BLOCK - LATE
ORDER = (0, 2, 1, 3)
SENT = 6
PER = 4
PARAMS = pltpu.CompilerParams(vmem_limit_bytes=48 * 1024 * 1024)
F32, BF16 = jnp.float32, jnp.bfloat16
NT = (((1,), (1,)), ((), ()))


def prototype():
    index = np.arange(TAPS * NCH, dtype=np.float64)
    window = 0.5 - 0.5 * np.cos(2.0 * math.pi * (index + 0.5) / (TAPS * NCH))
    taps = np.sinc((index + 0.5 - TAPS * NCH / 2) / NCH) * window
    return taps.astype(np.float32).reshape(TAPS, N1, N2)


def halves(table):
    high = table.astype(ml_dtypes.bfloat16)
    low = (table - high.astype(np.float64)).astype(ml_dtypes.bfloat16)
    return high, low


def complex_block(angle):
    c, s = np.cos(angle), np.sin(angle)
    return np.block([[c, s], [-s, c]])


def tables():
    k1, k2 = np.arange(N1), np.arange(N2)
    first = complex_block(2 * math.pi * (np.outer(k1, k1) % N1) / N1)
    second = complex_block(2 * math.pi * (np.outer(k2, k2) % N2) / N2) / 64.0
    second = second.reshape(2, ZH, Q, 8, 2 * N2).transpose(2, 1, 0, 3, 4).reshape(2 * N2, 2 * N2)
    turn = 2 * math.pi * np.outer(k1, k2) / NCH
    first = np.concatenate(halves(first), 0)
    second = np.concatenate(halves(second), 0)
    twiddle = np.stack([np.cos(turn), np.sin(turn)]).astype(np.float32)
    return first, second, twiddle


def spectrum(filtered, count, first, second, twiddle, stage, turned_re, turned_im, out):
    def pair(step, carry):
        for half in range(2):
            for r in range(2):
                stage[N1 * r : N1 * (r + 1), N2 * half : N2 * (half + 1)] = filtered(r, 2 * step + half).astype(BF16)
        both = jnp.dot(first[...], stage[...], preferred_element_type=F32)
        both = both[: 2 * N1] + both[2 * N1 :]
        for half in range(2):
            re = both[:N1, N2 * half : N2 * (half + 1)]
            im = both[N1:, N2 * half : N2 * (half + 1)]
            rows = pl.ds(2 * step + half, N1, stride=count)
            turned_re[rows, :] = re * twiddle[0] + im * twiddle[1]
            turned_im[rows, :] = im * twiddle[0] - re * twiddle[1]
        return carry

    lax.fori_loop(0, count // 2, pair, 0)
    for t in range(N1 * count // 256):
        rows = slice(256 * t, 256 * (t + 1))
        value = jnp.concatenate([turned_re[rows], turned_im[rows]], 1)
        high = value.astype(BF16)
        low = (value - high.astype(F32)).astype(BF16)
        both = lax.dot_general(second[...], high, NT, preferred_element_type=F32)
        rest = lax.dot_general(second[: 2 * N2], low, NT, preferred_element_type=F32)
        out[:, rows] = (both[: 2 * N2] + (both[2 * N2 :] + rest)).astype(BF16)


def early_body(core, column, station, *refs):
    pieces, refs = refs[:X], refs[X:]
    taps, first, second, twiddle, sums, out, frames, stage, turned_re, turned_im = refs
    start = BLOCK * core[0]
    for r in range(2):
        frames[r, :HIST] = jnp.zeros((HIST, N1, N2), F32)
        for piece, p in zip(pieces, ORDER):
            for d in range(2):
                shard = Q // X * ((column[0] + X - p) % X) + (core[0] + d) % 2
                frames[r, pl.ds(HIST + SENT * shard, SENT)] = piece[d, r].astype(F32)

    def filtered(r, f):
        acc = taps[0] * frames[r, start + f]
        for k in range(1, TAPS):
            acc = acc + taps[k] * frames[r, start + f + k]
        return acc

    def keep(f, carry):
        for r in range(2):
            sums[r, f] = filtered(r, f)
        return carry

    lax.fori_loop(0, FEW, keep, 0)
    late = lambda r, f: filtered(r, FEW + f)
    spectrum(late, LATE, first, second, twiddle, stage, turned_re, turned_im, out)


def rest_body(core, column, station, sums, hist, done, taps, first, second, twiddle, out, total, past, stage, turned_re, turned_im):
    out[:, N1 * FEW :] = done[...]
    total[...] = sums[...]

    @pl.when(core[0] == 0)
    def _():
        past[...] = hist[...].astype(F32)
        for f in range(HIST):
            for r in range(2):
                acc = sums[r, f]
                for k in range(HIST - f):
                    acc = acc + taps[k] * past[r, f + k]
                total[r, f] = acc

    spectrum(lambda r, f: total[r, f], FEW, first, second, twiddle, stage, turned_re, turned_im, out)


def kernel(body, scalars, args, out_shape, scratch, frames, name, interpret):
    vmem = pl.BlockSpec(memory_space=pltpu.VMEM)
    scratch = scratch + [
        pltpu.VMEM((2 * N1, 2 * N2), BF16),
        pltpu.VMEM((N1 * frames, N2), F32),
        pltpu.VMEM((N1 * frames, N2), F32),
    ]
    return pl.pallas_call(
        body,
        out_shape=out_shape,
        in_specs=[pl.BlockSpec(memory_space=pltpu.SMEM)] * len(scalars) + [vmem] * len(args),
        out_specs=jax.tree.map(lambda _: vmem, out_shape),
        scratch_shapes=scratch,
        compiler_params=PARAMS,
        interpret=interpret,
        name=name,
    )(*scalars, *args)


def channelise(scalars, pieces, hist, interpret=False):
    fixed = [jnp.asarray(a) for a in (prototype(), *tables())]
    shape = jax.ShapeDtypeStruct
    outs = (shape((2, FEW, N1, N2), F32), shape((2 * N2, N1 * LATE), BF16))
    scratch = [pltpu.VMEM((2, HIST + Q * SENT, N1, N2), F32)]
    sums, done = kernel(early_body, scalars, (*pieces, *fixed), outs, scratch, LATE, "early", interpret)
    outs = shape((2 * N2, N1 * BLOCK), BF16)
    scratch = [pltpu.VMEM((2, FEW, N1, N2), F32), pltpu.VMEM((2, HIST, N1, N2), F32)]
    return kernel(rest_body, scalars, (sums, hist, done, *fixed), outs, scratch, FEW, "rest", interpret)


def regroup_body(x, out):
    for z in range(ZH):
        pieces = []
        for c in range(2):
            for r in range(2):
                for i in range(PER):
                    pair = x[2 * i + c, 16 * z : 16 * z + 16, :].astype(F32)
                    pieces.append(pair[8 * r : 8 * r + 8])
        for t in range(N1 * BLOCK // 128):
            piece = jnp.concatenate([p[:, 128 * t : 128 * (t + 1)] for p in pieces], 0).T
            for part in range(16):
                k, f = divmod(128 * t + 8 * part, FEW)
                if k >= N1:
                    k, f = 16 * t + part - N1 * FEW // 8, FEW
                out[k, z, f : f + 8, :] = piece[8 * part : 8 * part + 8].astype(BF16)


def regroup(x, interpret=False):
    vmem = pl.BlockSpec(memory_space=pltpu.VMEM)
    return pl.pallas_call(
        regroup_body,
        out_shape=jax.ShapeDtypeStruct((STN, ZH, BLOCK, 128), BF16),
        in_specs=[vmem],
        out_specs=vmem,
        compiler_params=PARAMS,
        interpret=interpret,
        name="regroup",
    )(x)


def correlate_body(x, out, series, plain):
    most = jnp.zeros((8, 128), F32)
    zero = jnp.zeros((128 - FRAMES, 128), F32)
    for s in range(STN):
        both = jnp.concatenate([x[s, 0].astype(F32), x[s, 1].astype(F32)], 0)
        cols = jnp.concatenate([both, pltpu.roll(both, 64, 1), zero], 0)
        series[64 * s : 64 * (s + 1), :] = cols.T[:64]
    sign = jnp.where(lax.broadcasted_iota(jnp.int32, (STN, 8, 128), 1) < PER, 1.0, -1.0)
    for j in range(8):
        near = series[pl.ds(j, 8 * STN, stride=8), :].reshape(STN, 8, 128)
        far = (pltpu.roll(near, PER, 1) * sign).reshape(8 * STN, 128)
        left = jnp.concatenate([near.reshape(8 * STN, 128), far], 1).astype(BF16)
        right = []
        for r in range(2):
            rows = [series[pl.ds(32 * r + 8 * i + j, STN, stride=64), :] for i in range(PER)]
            right.append(jnp.concatenate(rows, 0))
        right = jnp.concatenate(right, 1).astype(BF16)
        tile = lax.dot_general(left, right, NT, preferred_element_type=F32) / FRAMES
        tile = tile.reshape(STN, 8, 128)
        plain[:, 8 * j : 8 * j + 8, :] = tile
        most = jnp.maximum(most, jnp.max(jnp.abs(tile), 0))
    top = jnp.max(jnp.max(most, 1, keepdims=True), 0, keepdims=True)
    power = jnp.maximum(jnp.floor(jnp.log2(jnp.maximum(top, 1e-37))) - 14.0, -126.0)
    factor, power = jnp.exp2(-power).reshape(1, 1, 1), power.reshape(1, 1, 1)
    station, row, lane = (lax.broadcasted_iota(jnp.int32, (STN, 8, 128), d) for d in range(3))
    out[:, :8, :] = jnp.where((row == 1) & (lane == station), power, plain[:, :8, :] * factor)
    out[:, 8:, :] = plain[:, 8:, :] * factor


def correlate(x, interpret=False):
    vmem = pl.BlockSpec(memory_space=pltpu.VMEM)
    return pl.pallas_call(
        correlate_body,
        out_shape=jax.ShapeDtypeStruct((STN, 64, 128), F32),
        in_specs=[vmem],
        out_specs=vmem,
        scratch_shapes=[pltpu.VMEM((64 * STN, 128), F32), pltpu.VMEM((STN, 64, 128), F32)],
        compiler_params=PARAMS,
        interpret=interpret,
        name="correlate",
    )(x)


def deliver_body(station, x, out, wide, order):
    here = x[:, :8, :]
    line, lane = (lax.broadcasted_iota(jnp.int32, (N1, 8, 128), d) for d in (1, 2))
    holder = (line == 1) & (lane == station[0])
    mirror = (line == 0) & (lane == station[0] + STN)

    def pick(mask):
        return jnp.sum(jnp.sum(jnp.where(mask, here, 0.0), 1, keepdims=True), 2, keepdims=True)

    factor = jnp.exp2(pick(holder))
    wide[...] = x[...] * factor
    wide[:, :8, :] = jnp.where(holder, pick(mirror), here) * factor
    flat = wide.reshape(64 * N1, 128)
    for row in range(8):
        for half in range(2):
            rows = [flat[pl.ds(8 * j + row, N1, stride=64), :] for j in range(4 * half, 4 * half + 4)]
            cols = jnp.concatenate(rows, 0).T
            base = 128 * (2 * row + half)
            for i in range(PER):
                order[pl.ds(base + i, STN, stride=PER), :] = cols[STN * i : STN * (i + 1)]
            out[row // PER, row % PER, :, 128 * half : 128 * (half + 1)] = order[base : base + 128, :]


def deliver(station, x, interpret=False):
    vmem = pl.BlockSpec(memory_space=pltpu.VMEM)
    return pl.pallas_call(
        deliver_body,
        out_shape=jax.ShapeDtypeStruct((2, PER, 128, 256), F32),
        in_specs=[pl.BlockSpec(memory_space=pltpu.SMEM), vmem],
        out_specs=vmem,
        scratch_shapes=[pltpu.VMEM((N1, 64, 128), F32), pltpu.VMEM((16 * 128, 128), F32)],
        compiler_params=PARAMS,
        interpret=interpret,
        name="deliver",
    )(station, x)


def last_frames(frames):
    q = Q // X * lax.axis_index("x") + lax.axis_index("c")
    rounds = []
    for r in range(X):
        piece = lax.dynamic_index_in_dim(frames, (q + r) % X, 1, False)
        pairs = [(s, Q // X * ((s + r) % X)) for s in range(Q - 3, Q)]
        rounds.append(lax.ppermute(piece, ("zh", "x", "c"), pairs))
    rounds = jnp.stack(rounds)
    parts = [
        lax.dynamic_index_in_dim(rounds, (lax.axis_index("x") - s) % X, 0, False) for s in range(Q - 3, Q)
    ]
    last = jnp.concatenate([parts[0][:, 3:], parts[1], parts[2]], 1)
    return lax.ppermute(last, ("zh", "x", "c"), [(Q // X * x, Q + Q // X * x) for x in range(X)])


def half_of_input(frames):
    other = lax.ppermute(frames, "c", [(0, 1), (1, 0)])
    pieces = []
    for p in ORDER:
        i = (lax.axis_index("x") + p) % X
        piece = jnp.stack([lax.dynamic_index_in_dim(a, i, 1, False) for a in (frames, other)])
        pairs = [(2 * x + c, 2 * ((x + p) % X) + c) for x in range(X) for c in range(2) if c or x < X // 2]
        pieces.append(lax.ppermute(piece, ("x", "c"), pairs) if p else piece)
    return pieces


def shards(voltages):
    frames = voltages.reshape(2, PER, SENT, N1, N2)
    hist = last_frames(frames)
    pieces = half_of_input(frames)
    scalars = [lax.axis_index(name).astype(jnp.int32).reshape(1) for name in ("c", "x", "stn")]
    spectra = channelise(scalars, pieces, hist)
    spectra = lax.all_to_all(spectra.reshape(Q, 2 * N2 // Q, N1 * BLOCK), ("x", "c"), 0, 0, tiled=True)
    spectra = regroup(spectra).reshape(STN * ZH, BLOCK, 128)
    spectra = lax.all_to_all(spectra, ("stn", "zh"), 0, 0, tiled=True)
    products = correlate(spectra.reshape(STN, ZH, BLOCK, 128))
    products = lax.all_to_all(products.astype(jnp.float16), "stn", 0, 0, tiled=True)
    return deliver(scalars[2], products.astype(F32))


def solution(mesh):
    split = Mesh(mesh.devices.reshape(STN, ZH, X, Q // X), ("stn", "zh", "x", "c"))
    in_specs = (P(None, "stn", ("zh", "x", "c")),)
    out_specs = P(None, "stn", None, ("zh", "x", "c"))
    return jax.shard_map(shards, mesh=split, in_specs=in_specs, out_specs=out_specs, check_vma=False)
```

```python
import math

import jax
import jax.numpy as jnp
import ml_dtypes
import numpy as np
from jax import lax
from jax.experimental import pallas as pl
from jax.experimental.pallas import tpu as pltpu
from jax.sharding import Mesh
from jax.sharding import PartitionSpec as P

TAPS = 16
NCH = 4096
N1, N2 = 32, 128
STN, ZH, X, Q = 32, 2, 4, 8
FRAMES = 96
BLOCK = 24
HIST = TAPS - 1
LATE = 8
FEW = BLOCK - LATE
ORDER = (0, 2, 1, 3)
SENT = 6
PER = 4
PARAMS = pltpu.CompilerParams(vmem_limit_bytes=48 * 1024 * 1024)
F32, BF16 = jnp.float32, jnp.bfloat16
NT = (((1,), (1,)), ((), ()))


def prototype():
    index = np.arange(TAPS * NCH, dtype=np.float64)
    window = 0.5 - 0.5 * np.cos(2.0 * math.pi * (index + 0.5) / (TAPS * NCH))
    taps = np.sinc((index + 0.5 - TAPS * NCH / 2) / NCH) * window
    return taps.astype(np.float32).reshape(TAPS, N1, N2)


def halves(table):
    high = table.astype(ml_dtypes.bfloat16)
    low = (table - high.astype(np.float64)).astype(ml_dtypes.bfloat16)
    return high, low


def complex_block(angle):
    c, s = np.cos(angle), np.sin(angle)
    return np.block([[c, s], [-s, c]])


def tables():
    k1, k2 = np.arange(N1), np.arange(N2)
    first = complex_block(2 * math.pi * (np.outer(k1, k1) % N1) / N1)
    second = complex_block(2 * math.pi * (np.outer(k2, k2) % N2) / N2) / 64.0
    second = second.reshape(2, ZH, Q, 8, 2 * N2).transpose(2, 1, 0, 3, 4).reshape(2 * N2, 2 * N2)
    turn = 2 * math.pi * np.outer(k1, k2) / NCH
    first = np.concatenate(halves(first), 0)
    second = np.concatenate(halves(second), 0)
    twiddle = np.stack([np.cos(turn), np.sin(turn)]).astype(np.float32)
    return first, second, twiddle


def spectrum(filtered, count, first, second, twiddle, stage, turned_re, turned_im, out):
    def pair(step, carry):
        for half in range(2):
            for r in range(2):
                stage[N1 * r : N1 * (r + 1), N2 * half : N2 * (half + 1)] = filtered(r, 2 * step + half).astype(BF16)
        both = jnp.dot(first[...], stage[...], preferred_element_type=F32)
        both = both[: 2 * N1] + both[2 * N1 :]
        for half in range(2):
            re = both[:N1, N2 * half : N2 * (half + 1)]
            im = both[N1:, N2 * half : N2 * (half + 1)]
            rows = pl.ds(2 * step + half, N1, stride=count)
            turned_re[rows, :] = re * twiddle[0] + im * twiddle[1]
            turned_im[rows, :] = im * twiddle[0] - re * twiddle[1]
        return carry

    lax.fori_loop(0, count // 2, pair, 0)
    for t in range(N1 * count // 256):
        rows = slice(256 * t, 256 * (t + 1))
        value = jnp.concatenate([turned_re[rows], turned_im[rows]], 1)
        high = value.astype(BF16)
        low = (value - high.astype(F32)).astype(BF16)
        both = lax.dot_general(second[...], high, NT, preferred_element_type=F32)
        rest = lax.dot_general(second[: 2 * N2], low, NT, preferred_element_type=F32)
        out[:, rows] = (both[: 2 * N2] + (both[2 * N2 :] + rest)).astype(BF16)


def early_body(core, column, station, *refs):
    pieces, refs = refs[:X], refs[X:]
    taps, first, second, twiddle, sums, out, frames, stage, turned_re, turned_im = refs
    start = BLOCK * core[0]
    for r in range(2):
        frames[r, :HIST] = jnp.zeros((HIST, N1, N2), F32)
        for piece, p in zip(pieces, ORDER):
            for d in range(2):
                shard = Q // X * ((column[0] + X - p) % X) + (core[0] + d) % 2
                frames[r, pl.ds(HIST + SENT * shard, SENT)] = piece[d, r].astype(F32)

    def filtered(r, f):
        acc = taps[0] * frames[r, start + f]
        for k in range(1, TAPS):
            acc = acc + taps[k] * frames[r, start + f + k]
        return acc

    def keep(f, carry):
        for r in range(2):
            sums[r, f] = filtered(r, f)
        return carry

    lax.fori_loop(0, FEW, keep, 0)
    late = lambda r, f: filtered(r, FEW + f)
    spectrum(late, LATE, first, second, twiddle, stage, turned_re, turned_im, out)


def rest_body(core, column, station, sums, hist, done, taps, first, second, twiddle, out, total, past, stage, turned_re, turned_im):
    out[:, N1 * FEW :] = done[...]
    total[...] = sums[...]

    @pl.when(core[0] == 0)
    def _():
        past[...] = hist[...].astype(F32)
        for f in range(HIST):
            for r in range(2):
                acc = sums[r, f]
                for k in range(HIST - f):
                    acc = acc + taps[k] * past[r, f + k]
                total[r, f] = acc

    spectrum(lambda r, f: total[r, f], FEW, first, second, twiddle, stage, turned_re, turned_im, out)


def kernel(body, scalars, args, out_shape, scratch, frames, name, interpret):
    vmem = pl.BlockSpec(memory_space=pltpu.VMEM)
    scratch = scratch + [
        pltpu.VMEM((2 * N1, 2 * N2), BF16),
        pltpu.VMEM((N1 * frames, N2), F32),
        pltpu.VMEM((N1 * frames, N2), F32),
    ]
    return pl.pallas_call(
        body,
        out_shape=out_shape,
        in_specs=[pl.BlockSpec(memory_space=pltpu.SMEM)] * len(scalars) + [vmem] * len(args),
        out_specs=jax.tree.map(lambda _: vmem, out_shape),
        scratch_shapes=scratch,
        compiler_params=PARAMS,
        interpret=interpret,
        name=name,
    )(*scalars, *args)


def channelise(scalars, pieces, hist, interpret=False):
    fixed = [jnp.asarray(a) for a in (prototype(), *tables())]
    shape = jax.ShapeDtypeStruct
    outs = (shape((2, FEW, N1, N2), F32), shape((2 * N2, N1 * LATE), BF16))
    scratch = [pltpu.VMEM((2, HIST + Q * SENT, N1, N2), F32)]
    sums, done = kernel(early_body, scalars, (*pieces, *fixed), outs, scratch, LATE, "early", interpret)
    outs = shape((2 * N2, N1 * BLOCK), BF16)
    scratch = [pltpu.VMEM((2, FEW, N1, N2), F32), pltpu.VMEM((2, HIST, N1, N2), F32)]
    return kernel(rest_body, scalars, (sums, hist, done, *fixed), outs, scratch, FEW, "rest", interpret)


def regroup_body(x, out):
    for z in range(ZH):
        pieces = []
        for c in range(2):
            for r in range(2):
                for i in range(PER):
                    pair = x[2 * i + c, 16 * z : 16 * z + 16, :].astype(F32)
                    pieces.append(pair[8 * r : 8 * r + 8])
        for t in range(N1 * BLOCK // 128):
            piece = jnp.concatenate([p[:, 128 * t : 128 * (t + 1)] for p in pieces], 0).T
            for part in range(16):
                k, f = divmod(128 * t + 8 * part, FEW)
                if k >= N1:
                    k, f = 16 * t + part - N1 * FEW // 8, FEW
                out[k, z, f : f + 8, :] = piece[8 * part : 8 * part + 8].astype(BF16)


def regroup(x, interpret=False):
    vmem = pl.BlockSpec(memory_space=pltpu.VMEM)
    return pl.pallas_call(
        regroup_body,
        out_shape=jax.ShapeDtypeStruct((STN, ZH, BLOCK, 128), BF16),
        in_specs=[vmem],
        out_specs=vmem,
        compiler_params=PARAMS,
        interpret=interpret,
        name="regroup",
    )(x)


def correlate_body(x, out, series, plain):
    most = jnp.zeros((8, 128), F32)
    zero = jnp.zeros((128 - FRAMES, 128), F32)
    for s in range(STN):
        both = jnp.concatenate([x[s, 0].astype(F32), x[s, 1].astype(F32)], 0)
        cols = jnp.concatenate([both, pltpu.roll(both, 64, 1), zero], 0)
        series[64 * s : 64 * (s + 1), :] = cols.T[:64]
    sign = jnp.where(lax.broadcasted_iota(jnp.int32, (STN, 8, 128), 1) < PER, 1.0, -1.0)
    for j in range(8):
        near = series[pl.ds(j, 8 * STN, stride=8), :].reshape(STN, 8, 128)
        far = (pltpu.roll(near, PER, 1) * sign).reshape(8 * STN, 128)
        left = jnp.concatenate([near.reshape(8 * STN, 128), far], 1).astype(BF16)
        right = []
        for r in range(2):
            rows = [series[pl.ds(32 * r + 8 * i + j, STN, stride=64), :] for i in range(PER)]
            right.append(jnp.concatenate(rows, 0))
        right = jnp.concatenate(right, 1).astype(BF16)
        tile = lax.dot_general(left, right, NT, preferred_element_type=F32) / FRAMES
        tile = tile.reshape(STN, 8, 128)
        plain[:, 8 * j : 8 * j + 8, :] = tile
        most = jnp.maximum(most, jnp.max(jnp.abs(tile), 0))
    top = jnp.max(jnp.max(most, 1, keepdims=True), 0, keepdims=True)
    power = jnp.maximum(jnp.floor(jnp.log2(jnp.maximum(top, 1e-37))) - 14.0, -126.0)
    factor, power = jnp.exp2(-power).reshape(1, 1, 1), power.reshape(1, 1, 1)
    station, row, lane = (lax.broadcasted_iota(jnp.int32, (STN, 8, 128), d) for d in range(3))
    out[:, :8, :] = jnp.where((row == 1) & (lane == station), power, plain[:, :8, :] * factor)
    out[:, 8:, :] = plain[:, 8:, :] * factor


def correlate(x, interpret=False):
    vmem = pl.BlockSpec(memory_space=pltpu.VMEM)
    return pl.pallas_call(
        correlate_body,
        out_shape=jax.ShapeDtypeStruct((STN, 64, 128), F32),
        in_specs=[vmem],
        out_specs=vmem,
        scratch_shapes=[pltpu.VMEM((64 * STN, 128), F32), pltpu.VMEM((STN, 64, 128), F32)],
        compiler_params=PARAMS,
        interpret=interpret,
        name="correlate",
    )(x)


def deliver_body(station, x, out, wide, order):
    here = x[:, :8, :]
    line, lane = (lax.broadcasted_iota(jnp.int32, (N1, 8, 128), d) for d in (1, 2))
    holder = (line == 1) & (lane == station[0])
    mirror = (line == 0) & (lane == station[0] + STN)

    def pick(mask):
        return jnp.sum(jnp.sum(jnp.where(mask, here, 0.0), 1, keepdims=True), 2, keepdims=True)

    factor = jnp.exp2(pick(holder))
    wide[...] = x[...] * factor
    wide[:, :8, :] = jnp.where(holder, pick(mirror), here) * factor
    flat = wide.reshape(64 * N1, 128)
    for row in range(8):
        for half in range(2):
            rows = [flat[pl.ds(8 * j + row, N1, stride=64), :] for j in range(4 * half, 4 * half + 4)]
            cols = jnp.concatenate(rows, 0).T
            base = 128 * (2 * row + half)
            for i in range(PER):
                order[pl.ds(base + i, STN, stride=PER), :] = cols[STN * i : STN * (i + 1)]
            out[row // PER, row % PER, :, 128 * half : 128 * (half + 1)] = order[base : base + 128, :]


def deliver(station, x, interpret=False):
    vmem = pl.BlockSpec(memory_space=pltpu.VMEM)
    return pl.pallas_call(
        deliver_body,
        out_shape=jax.ShapeDtypeStruct((2, PER, 128, 256), F32),
        in_specs=[pl.BlockSpec(memory_space=pltpu.SMEM), vmem],
        out_specs=vmem,
        scratch_shapes=[pltpu.VMEM((N1, 64, 128), F32), pltpu.VMEM((16 * 128, 128), F32)],
        compiler_params=PARAMS,
        interpret=interpret,
        name="deliver",
    )(station, x)


def last_frames(frames):
    q = Q // X * lax.axis_index("x") + lax.axis_index("c")
    rounds = []
    for r in range(X):
        piece = lax.dynamic_index_in_dim(frames, (q + r) % X, 1, False)
        pairs = [(s, Q // X * ((s + r) % X)) for s in range(Q - 3, Q)]
        rounds.append(lax.ppermute(piece, ("zh", "x", "c"), pairs))
    rounds = jnp.stack(rounds)
    parts = [
        lax.dynamic_index_in_dim(rounds, (lax.axis_index("x") - s) % X, 0, False) for s in range(Q - 3, Q)
    ]
    last = jnp.concatenate([parts[0][:, 3:], parts[1], parts[2]], 1)
    return lax.ppermute(last, ("zh", "x", "c"), [(Q // X * x, Q + Q // X * x) for x in range(X)])


def half_of_input(frames):
    swap = [(2 * x + c, 2 * x + 1 - c) for x in range(X) for c in range(2) if not c or x < X // 2]
    other = lax.ppermute(frames, ("x", "c"), swap)
    pieces = []
    for p in ORDER:
        i = (lax.axis_index("x") + p) % X
        piece = jnp.stack([lax.dynamic_index_in_dim(a, i, 1, False) for a in (frames, other)])
        pairs = [(2 * x + c, 2 * ((x + p) % X) + c) for x in range(X) for c in range(2) if c or x < X // 2]
        pieces.append(lax.ppermute(piece, ("x", "c"), pairs) if p else piece)
    return pieces


def shards(voltages):
    frames = voltages.reshape(2, PER, SENT, N1, N2)
    hist = last_frames(frames)
    pieces = half_of_input(frames)
    scalars = [lax.axis_index(name).astype(jnp.int32).reshape(1) for name in ("c", "x", "stn")]
    spectra = channelise(scalars, pieces, hist)
    spectra = lax.all_to_all(spectra.reshape(Q, 2 * N2 // Q, N1 * BLOCK), ("x", "c"), 0, 0, tiled=True)
    spectra = regroup(spectra).reshape(STN * ZH, BLOCK, 128)
    spectra = lax.all_to_all(spectra, ("stn", "zh"), 0, 0, tiled=True)
    products = correlate(spectra.reshape(STN, ZH, BLOCK, 128))
    products = lax.all_to_all(products.astype(jnp.float16), "stn", 0, 0, tiled=True)
    return deliver(scalars[2], products.astype(F32))


def solution(mesh):
    split = Mesh(mesh.devices.reshape(STN, ZH, X, Q // X), ("stn", "zh", "x", "c"))
    in_specs = (P(None, "stn", ("zh", "x", "c")),)
    out_specs = P(None, "stn", None, ("zh", "x", "c"))
    return jax.shard_map(shards, mesh=split, in_specs=in_specs, out_specs=out_specs, check_vma=False)
```

```python
import math

import jax
import jax.numpy as jnp
import ml_dtypes
import numpy as np
from jax import lax
from jax.experimental import pallas as pl
from jax.experimental.pallas import tpu as pltpu
from jax.sharding import Mesh
from jax.sharding import PartitionSpec as P

TAPS = 16
NCH = 4096
N1, N2 = 32, 128
STN, ZH, X, Q = 32, 2, 4, 8
FRAMES = 96
BLOCK = 24
HIST = TAPS - 1
LATE = 8
FEW = BLOCK - LATE
ORDER = (0, 2, 1, 3)
SENT = 6
PER = 4
PARAMS = pltpu.CompilerParams(vmem_limit_bytes=48 * 1024 * 1024)
F32, BF16 = jnp.float32, jnp.bfloat16
NT = (((1,), (1,)), ((), ()))


def prototype():
    index = np.arange(TAPS * NCH, dtype=np.float64)
    window = 0.5 - 0.5 * np.cos(2.0 * math.pi * (index + 0.5) / (TAPS * NCH))
    taps = np.sinc((index + 0.5 - TAPS * NCH / 2) / NCH) * window
    return taps.astype(np.float32).reshape(TAPS, N1, N2)


def halves(table):
    high = table.astype(ml_dtypes.bfloat16)
    low = (table - high.astype(np.float64)).astype(ml_dtypes.bfloat16)
    return high, low


def complex_block(angle):
    c, s = np.cos(angle), np.sin(angle)
    return np.block([[c, s], [-s, c]])


def tables():
    k1, k2 = np.arange(N1), np.arange(N2)
    first = complex_block(2 * math.pi * (np.outer(k1, k1) % N1) / N1)
    second = complex_block(2 * math.pi * (np.outer(k2, k2) % N2) / N2) / 64.0
    second = second.reshape(2, ZH, Q, 8, 2 * N2).transpose(2, 1, 0, 3, 4).reshape(2 * N2, 2 * N2)
    turn = 2 * math.pi * np.outer(k1, k2) / NCH
    first = np.concatenate(halves(first), 0)
    second = np.concatenate(halves(second), 0)
    twiddle = np.stack([np.cos(turn), np.sin(turn)]).astype(np.float32)
    return first, second, twiddle


def spectrum(filtered, count, first, second, twiddle, stage, turned_re, turned_im, out):
    def pair(step, carry):
        for half in range(2):
            for r in range(2):
                stage[N1 * r : N1 * (r + 1), N2 * half : N2 * (half + 1)] = filtered(r, 2 * step + half).astype(BF16)
        both = jnp.dot(first[...], stage[...], preferred_element_type=F32)
        both = both[: 2 * N1] + both[2 * N1 :]
        for half in range(2):
            re = both[:N1, N2 * half : N2 * (half + 1)]
            im = both[N1:, N2 * half : N2 * (half + 1)]
            rows = pl.ds(2 * step + half, N1, stride=count)
            turned_re[rows, :] = re * twiddle[0] + im * twiddle[1]
            turned_im[rows, :] = im * twiddle[0] - re * twiddle[1]
        return carry

    lax.fori_loop(0, count // 2, pair, 0)
    for t in range(N1 * count // 256):
        rows = slice(256 * t, 256 * (t + 1))
        value = jnp.concatenate([turned_re[rows], turned_im[rows]], 1)
        high = value.astype(BF16)
        low = (value - high.astype(F32)).astype(BF16)
        both = lax.dot_general(second[...], high, NT, preferred_element_type=F32)
        rest = lax.dot_general(second[: 2 * N2], low, NT, preferred_element_type=F32)
        out[:, rows] = (both[: 2 * N2] + (both[2 * N2 :] + rest)).astype(BF16)


def early_body(core, column, station, *refs):
    pieces, refs = refs[:X], refs[X:]
    taps, first, second, twiddle, sums, out, frames, stage, turned_re, turned_im = refs
    start = BLOCK * core[0]
    for r in range(2):
        frames[r, :HIST] = jnp.zeros((HIST, N1, N2), F32)
        for piece, p in zip(pieces, ORDER):
            for d in range(2):
                shard = Q // X * ((column[0] + X - p) % X) + (core[0] + d) % 2
                frames[r, pl.ds(HIST + SENT * shard, SENT)] = piece[d, r].astype(F32)

    def filtered(r, f):
        acc = taps[0] * frames[r, start + f]
        for k in range(1, TAPS):
            acc = acc + taps[k] * frames[r, start + f + k]
        return acc

    def keep(f, carry):
        for r in range(2):
            sums[r, f] = filtered(r, f)
        return carry

    lax.fori_loop(0, FEW, keep, 0)
    late = lambda r, f: filtered(r, FEW + f)
    spectrum(late, LATE, first, second, twiddle, stage, turned_re, turned_im, out)


def rest_body(core, column, station, sums, hist, done, taps, first, second, twiddle, out, total, past, stage, turned_re, turned_im):
    out[:, N1 * FEW :] = done[...]
    total[...] = sums[...]

    @pl.when(core[0] == 0)
    def _():
        past[...] = hist[...].astype(F32)
        for f in range(HIST):
            for r in range(2):
                acc = sums[r, f]
                for k in range(HIST - f):
                    acc = acc + taps[k] * past[r, f + k]
                total[r, f] = acc

    spectrum(lambda r, f: total[r, f], FEW, first, second, twiddle, stage, turned_re, turned_im, out)


def kernel(body, scalars, args, out_shape, scratch, frames, name, interpret):
    vmem = pl.BlockSpec(memory_space=pltpu.VMEM)
    scratch = scratch + [
        pltpu.VMEM((2 * N1, 2 * N2), BF16),
        pltpu.VMEM((N1 * frames, N2), F32),
        pltpu.VMEM((N1 * frames, N2), F32),
    ]
    return pl.pallas_call(
        body,
        out_shape=out_shape,
        in_specs=[pl.BlockSpec(memory_space=pltpu.SMEM)] * len(scalars) + [vmem] * len(args),
        out_specs=jax.tree.map(lambda _: vmem, out_shape),
        scratch_shapes=scratch,
        compiler_params=PARAMS,
        interpret=interpret,
        name=name,
    )(*scalars, *args)


def channelise(scalars, pieces, hist, interpret=False):
    fixed = [jnp.asarray(a) for a in (prototype(), *tables())]
    shape = jax.ShapeDtypeStruct
    outs = (shape((2, FEW, N1, N2), F32), shape((2 * N2, N1 * LATE), BF16))
    scratch = [pltpu.VMEM((2, HIST + Q * SENT, N1, N2), F32)]
    sums, done = kernel(early_body, scalars, (*pieces, *fixed), outs, scratch, LATE, "early", interpret)
    outs = shape((2 * N2, N1 * BLOCK), BF16)
    scratch = [pltpu.VMEM((2, FEW, N1, N2), F32), pltpu.VMEM((2, HIST, N1, N2), F32)]
    return kernel(rest_body, scalars, (sums, hist, done, *fixed), outs, scratch, FEW, "rest", interpret)


def regroup_body(x, out):
    for z in range(ZH):
        pieces = []
        for c in range(2):
            for r in range(2):
                for i in range(PER):
                    pair = x[2 * i + c, 16 * z : 16 * z + 16, :].astype(F32)
                    pieces.append(pair[8 * r : 8 * r + 8])
        for t in range(N1 * BLOCK // 128):
            piece = jnp.concatenate([p[:, 128 * t : 128 * (t + 1)] for p in pieces], 0).T
            for part in range(16):
                k, f = divmod(128 * t + 8 * part, FEW)
                if k >= N1:
                    k, f = 16 * t + part - N1 * FEW // 8, FEW
                out[k, z, f : f + 8, :] = piece[8 * part : 8 * part + 8].astype(BF16)


def regroup(x, interpret=False):
    vmem = pl.BlockSpec(memory_space=pltpu.VMEM)
    return pl.pallas_call(
        regroup_body,
        out_shape=jax.ShapeDtypeStruct((STN, ZH, BLOCK, 128), BF16),
        in_specs=[vmem],
        out_specs=vmem,
        compiler_params=PARAMS,
        interpret=interpret,
        name="regroup",
    )(x)


def correlate_body(x, out, series, plain):
    most = jnp.zeros((8, 128), F32)
    zero = jnp.zeros((128 - FRAMES, 128), F32)
    for s in range(STN):
        both = jnp.concatenate([x[s, 0].astype(F32), x[s, 1].astype(F32)], 0)
        cols = jnp.concatenate([both, pltpu.roll(both, 64, 1), zero], 0)
        series[64 * s : 64 * (s + 1), :] = cols.T[:64]
    sign = jnp.where(lax.broadcasted_iota(jnp.int32, (STN, 8, 128), 1) < PER, 1.0, -1.0)
    for j in range(8):
        near = series[pl.ds(j, 8 * STN, stride=8), :].reshape(STN, 8, 128)
        far = (pltpu.roll(near, PER, 1) * sign).reshape(8 * STN, 128)
        left = jnp.concatenate([near.reshape(8 * STN, 128), far], 1).astype(BF16)
        right = []
        for r in range(2):
            rows = [series[pl.ds(32 * r + 8 * i + j, STN, stride=64), :] for i in range(PER)]
            right.append(jnp.concatenate(rows, 0))
        right = jnp.concatenate(right, 1).astype(BF16)
        tile = lax.dot_general(left, right, NT, preferred_element_type=F32) * (1.0 / FRAMES)
        tile = tile.reshape(STN, 8, 128)
        plain[:, 8 * j : 8 * j + 8, :] = tile
        most = jnp.maximum(most, jnp.max(jnp.abs(tile), 0))
    top = jnp.max(jnp.max(most, 1, keepdims=True), 0, keepdims=True)
    power = jnp.maximum(jnp.floor(jnp.log2(jnp.maximum(top, 1e-37))) - 14.0, -126.0)
    factor, power = jnp.exp2(-power).reshape(1, 1, 1), power.reshape(1, 1, 1)
    station, row, lane = (lax.broadcasted_iota(jnp.int32, (STN, 8, 128), d) for d in range(3))
    out[:, :8, :] = jnp.where((row == 1) & (lane == station), power, plain[:, :8, :] * factor)
    out[:, 8:, :] = plain[:, 8:, :] * factor


def correlate(x, interpret=False):
    vmem = pl.BlockSpec(memory_space=pltpu.VMEM)
    return pl.pallas_call(
        correlate_body,
        out_shape=jax.ShapeDtypeStruct((STN, 64, 128), F32),
        in_specs=[vmem],
        out_specs=vmem,
        scratch_shapes=[pltpu.VMEM((64 * STN, 128), F32), pltpu.VMEM((STN, 64, 128), F32)],
        compiler_params=PARAMS,
        interpret=interpret,
        name="correlate",
    )(x)


def deliver_body(station, x, out, wide, order):
    here = x[:, :8, :]
    line, lane = (lax.broadcasted_iota(jnp.int32, (N1, 8, 128), d) for d in (1, 2))
    holder = (line == 1) & (lane == station[0])
    mirror = (line == 0) & (lane == station[0] + STN)

    def pick(mask):
        return jnp.sum(jnp.sum(jnp.where(mask, here, 0.0), 1, keepdims=True), 2, keepdims=True)

    factor = jnp.exp2(pick(holder))
    wide[...] = x[...] * factor
    wide[:, :8, :] = jnp.where(holder, pick(mirror), here) * factor
    flat = wide.reshape(64 * N1, 128)
    for row in range(8):
        for half in range(2):
            rows = [flat[pl.ds(8 * j + row, N1, stride=64), :] for j in range(4 * half, 4 * half + 4)]
            cols = jnp.concatenate(rows, 0).T
            base = 128 * (2 * row + half)
            for i in range(PER):
                order[pl.ds(base + i, STN, stride=PER), :] = cols[STN * i : STN * (i + 1)]
            out[row // PER, row % PER, :, 128 * half : 128 * (half + 1)] = order[base : base + 128, :]


def deliver(station, x, interpret=False):
    vmem = pl.BlockSpec(memory_space=pltpu.VMEM)
    return pl.pallas_call(
        deliver_body,
        out_shape=jax.ShapeDtypeStruct((2, PER, 128, 256), F32),
        in_specs=[pl.BlockSpec(memory_space=pltpu.SMEM), vmem],
        out_specs=vmem,
        scratch_shapes=[pltpu.VMEM((N1, 64, 128), F32), pltpu.VMEM((16 * 128, 128), F32)],
        compiler_params=PARAMS,
        interpret=interpret,
        name="deliver",
    )(station, x)


def last_frames(frames):
    q = Q // X * lax.axis_index("x") + lax.axis_index("c")
    rounds = []
    for r in range(X):
        piece = lax.dynamic_index_in_dim(frames, (q + r) % X, 1, False)
        pairs = [(s, Q // X * ((s + r) % X)) for s in range(Q - 3, Q)]
        rounds.append(lax.ppermute(piece, ("zh", "x", "c"), pairs))
    rounds = jnp.stack(rounds)
    parts = [
        lax.dynamic_index_in_dim(rounds, (lax.axis_index("x") - s) % X, 0, False) for s in range(Q - 3, Q)
    ]
    last = jnp.concatenate([parts[0][:, 3:], parts[1], parts[2]], 1)
    return lax.ppermute(last, ("zh", "x", "c"), [(Q // X * x, Q + Q // X * x) for x in range(X)])


def half_of_input(frames):
    swap = [(2 * x + c, 2 * x + 1 - c) for x in range(X) for c in range(2) if not c or x < X // 2]
    other = lax.ppermute(frames, ("x", "c"), swap)
    pieces = []
    for p in ORDER:
        i = (lax.axis_index("x") + p) % X
        piece = jnp.stack([lax.dynamic_index_in_dim(a, i, 1, False) for a in (frames, other)])
        pairs = [(2 * x + c, 2 * ((x + p) % X) + c) for x in range(X) for c in range(2) if c or x < X // 2]
        pieces.append(lax.ppermute(piece, ("x", "c"), pairs) if p else piece)
    return pieces


def shards(voltages):
    frames = voltages.reshape(2, PER, SENT, N1, N2)
    hist = last_frames(frames)
    pieces = half_of_input(frames)
    scalars = [lax.axis_index(name).astype(jnp.int32).reshape(1) for name in ("c", "x", "stn")]
    spectra = channelise(scalars, pieces, hist)
    spectra = lax.all_to_all(spectra.reshape(Q, 2 * N2 // Q, N1 * BLOCK), ("x", "c"), 0, 0, tiled=True)
    spectra = regroup(spectra).reshape(STN * ZH, BLOCK, 128)
    spectra = lax.all_to_all(spectra, ("stn", "zh"), 0, 0, tiled=True)
    products = correlate(spectra.reshape(STN, ZH, BLOCK, 128))
    products = lax.all_to_all(products.astype(jnp.float16), "stn", 0, 0, tiled=True)
    return deliver(scalars[2], products.astype(F32))


def solution(mesh):
    split = Mesh(mesh.devices.reshape(STN, ZH, X, Q // X), ("stn", "zh", "x", "c"))
    in_specs = (P(None, "stn", ("zh", "x", "c")),)
    out_specs = P(None, "stn", None, ("zh", "x", "c"))
    return jax.shard_map(shards, mesh=split, in_specs=in_specs, out_specs=out_specs, check_vma=False)
```
